32 devices in a mesh: seq: 8 (over z, y), trk: 4 (over x, core).
Axes of the slice: x: 2, y: 2, z: 4, core: 2. Of those that a mesh axis runs over, the one named last changes fastest.
Arguments:
- bins: bfloat16 [8192, 768], P(('seq', 'trk')), may hold values from -6.7 to 6.7
- species: int32 [8], replicated, may hold values from 0 to 1, as said below
- cot_human: bfloat16 [8192, 5313], P(('seq', 'trk')), may hold values from -6.7 to 6.7
- cot_mouse: bfloat16 [8192, 1643], P(('seq', 'trk')), may hold values from -6.7 to 6.7
- norm_params: float32 [2304], P(('seq', 'trk')), may hold values from -1.6 to 1.6
- norm_first: float32 [2304], P(('seq', 'trk')), may hold values from -32 to 32
- norm_second: float32 [2304], P(('seq', 'trk')), may hold values from 2.048 to 8.192
- dilated_weight: float32 [3, 768, 384], P(None, ('seq', 'trk')), may hold values from -0.13958333 to 0.13958333
- dilated_first: float32 [3, 768, 384], P(None, ('seq', 'trk')), may hold values from -20.817224 to 20.817224
- dilated_second: float32 [3, 768, 384], P(None, ('seq', 'trk')), may hold values from 0.73728 to 2.94912
- point_weight: float32 [384, 768], P(None, ('seq', 'trk')), may hold values from -0.5460321 to 0.5460321
- point_first: float32 [384, 768], P(None, ('seq', 'trk')), may hold values from -20.817224 to 20.817224
- point_second: float32 [384, 768], P(None, ('seq', 'trk')), may hold values from 0.73728 to 2.94912
- final_weight: float32 [768, 1536], P(None, ('seq', 'trk')), may hold values from -0.40414519 to 0.40414519
- final_first: float32 [768, 1536], P(None, ('seq', 'trk')), may hold values from -33.48858 to 33.48858
- final_second: float32 [768, 1536], P(None, ('seq', 'trk')), may hold values from 0.73728 to 2.94912
- human_weight: float32 [1536, 5313], P(('seq', 'trk')), may hold values from -0.2857738 to 0.2857738
- human_first: float32 [1536, 5313], P(('seq', 'trk')), may hold values from -22.627417 to 22.627417
- human_second: float32 [1536, 5313], P(('seq', 'trk')), may hold values from 0.32768 to 1.31072
- mouse_weight: float32 [1536, 1643], P(('seq', 'trk')), may hold values from -0.2857738 to 0.2857738
- mouse_first: float32 [1536, 1643], P(('seq', 'trk')), may hold values from -22.627417 to 22.627417
- mouse_second: float32 [1536, 1643], P(('seq', 'trk')), may hold values from 0.32768 to 1.31072
Outputs:
- human_output: float32 [8192, 5313], P(('seq', 'trk'))
- mouse_output: float32 [8192, 1643], P(('seq', 'trk'))
- input_grad: float32 [8192, 768], P(('seq', 'trk'))
- norm_momentum: float32 [2304], P(('seq', 'trk'))
- norm_variance: float32 [2304], P(('seq', 'trk'))
- norm_updated: float32 [2304], P(('seq', 'trk'))
- dilated_momentum: float32 [3, 768, 384], P(None, ('seq', 'trk'))
- dilated_variance: float32 [3, 768, 384], P(None, ('seq', 'trk'))
- dilated_updated: float32 [3, 768, 384], P(None, ('seq', 'trk'))
- point_momentum: float32 [384, 768], P(None, ('seq', 'trk'))
- point_variance: float32 [384, 768], P(None, ('seq', 'trk'))
- point_updated: float32 [384, 768], P(None, ('seq', 'trk'))
- final_momentum: float32 [768, 1536], P(None, ('seq', 'trk'))
- final_variance: float32 [768, 1536], P(None, ('seq', 'trk'))
- final_updated: float32 [768, 1536], P(None, ('seq', 'trk'))
- human_momentum: float32 [1536, 5313], P(('seq', 'trk'))
- human_variance: float32 [1536, 5313], P(('seq', 'trk'))
- human_updated: float32 [1536, 5313], P(('seq', 'trk'))
- mouse_momentum: float32 [1536, 1643], P(('seq', 'trk'))
- mouse_variance: float32 [1536, 1643], P(('seq', 'trk'))
- mouse_updated: float32 [1536, 1643], P(('seq', 'trk'))
- trust_stats: float32 [3, 5], replicated
The draws below stay inside these ranges and needn't reach their ends.
Inputs may be any that keep to these rules, and one draw needn't show every extreme that they name: Both species occur.
All inputs are finite; a program needn't handle non-finite values.
Results may differ from the reference program's by a relative error of at most 0.01.
The reference program's roundings to bfloat16 on the way count: a program that leaves them out, or rounds other values in their place, can miss the bound.
Values may be sent and summed in bfloat16 or wider, within the bound.
No kernel may reach another device: no remote copies, remote signals or barrier semaphores. Data moves between devices by JAX's collectives and lax.ppermute only.
A program may use at most 192 MiB of HBM per device.

```python
import math
import jax
import jax.numpy as jnp
from jax import lax

C = 768
B = 384
F = 1536
HT = 5313
MT = 1643
DILATION_GAP = 57
WINDOW_BINS = 1024
STEP = 10
BINS = 8192
WINDOWS = 8
NP = 2304


def ramped(key, shape, scale, dims, top):
    normal_part = jnp.clip(jax.random.normal(jax.random.fold_in(key, 1), shape, jnp.float32), -4.0, 4.0)
    values = normal_part
    for dim_index in dims:
        count = shape[dim_index]
        fraction = jnp.arange(count, dtype=jnp.float32) / max(count - 1, 1)
        profile = (1.0 + (top - 1.0) * fraction) * (2.0 / (1.0 + top))
        layout = [1] * len(shape)
        layout[dim_index] = count
        values = values * profile.reshape(layout)
    return scale * values


def draw_bins(key, part):
    key = jax.random.fold_in(key, 21)
    top = 3.0
    return ramped(key, (BINS, C), 1.0, (0,), top).astype(jnp.bfloat16)


def draw_species(key, part):
    key = jax.random.fold_in(key, 22)
    flags = jax.random.randint(jax.random.fold_in(key, 1), (WINDOWS,), 0, 2)
    first_pick = jax.random.randint(jax.random.fold_in(key, 2), (), 0, WINDOWS)
    second_pick = (first_pick + 1 + jax.random.randint(jax.random.fold_in(key, 3), (), 0, WINDOWS - 1)) % WINDOWS
    tap_positions = jnp.arange(WINDOWS)
    flags = jnp.where(tap_positions == first_pick, 0, flags)
    flags = jnp.where(tap_positions == second_pick, 1, flags)
    return flags.astype(jnp.int32)


def draw_cot_human(key, part):
    key = jax.random.fold_in(key, 23)
    top = 3.0
    return ramped(key, (BINS, HT), 1.0, (1,), top).astype(jnp.bfloat16)


def draw_cot_mouse(key, part):
    key = jax.random.fold_in(key, 24)
    top = 3.0
    return ramped(key, (BINS, MT), 1.0, (1,), top).astype(jnp.bfloat16)


def draw_norm_params(key, part):
    key = jax.random.fold_in(key, 25)
    top = 3.0
    gain_one = 1.0 + 0.15 * ramped(jax.random.fold_in(key, 5), (C,), 1.0, (), top)
    shift_one = 0.4 * ramped(jax.random.fold_in(key, 6), (C,), 1.0, (), top)
    gain_two = 1.0 + 0.15 * ramped(jax.random.fold_in(key, 7), (B,), 1.0, (), top)
    shift_two = 0.4 * ramped(jax.random.fold_in(key, 8), (B,), 1.0, (), top)
    return jnp.concatenate([gain_one, shift_one, gain_two, shift_two])


def draw_dilated_weight(key, part):
    key = jax.random.fold_in(key, 26)
    top = 3.0
    return ramped(key, (3, C, B), (3 * C) ** (-0.5), (1,), top)


def draw_dilated_first(key, part):
    key = jax.random.fold_in(key, 27)
    top = 3.0
    return ramped(key, (3, C, B), 0.033 * BINS ** 0.5, (1,), top)


def draw_point_weight(key, part):
    key = jax.random.fold_in(key, 28)
    top = 3.0
    return ramped(key, (B, C), 1.6 * B ** (-0.5), (0,), top)


def draw_point_first(key, part):
    key = jax.random.fold_in(key, 29)
    top = 3.0
    return ramped(key, (B, C), 0.033 * BINS ** 0.5, (0,), top)


def draw_final_weight(key, part):
    key = jax.random.fold_in(key, 30)
    top = 3.0
    return ramped(key, (C, F), C ** (-0.5), (0, 1), top)


def draw_final_first(key, part):
    key = jax.random.fold_in(key, 31)
    top = 3.0
    return ramped(key, (C, F), 0.033 * BINS ** 0.5, (0, 1), top)


def draw_human_weight(key, part):
    key = jax.random.fold_in(key, 32)
    top = 3.0
    return ramped(key, (F, HT), F ** (-0.5), (0, 1), top)


def draw_human_first(key, part):
    key = jax.random.fold_in(key, 33)
    top = 3.0
    return ramped(key, (F, HT), 0.022 * BINS ** 0.5, (0, 1), top)


def draw_mouse_weight(key, part):
    key = jax.random.fold_in(key, 34)
    top = 3.0
    return ramped(key, (F, MT), F ** (-0.5), (0, 1), top)


def draw_mouse_first(key, part):
    key = jax.random.fold_in(key, 35)
    top = 3.0
    return ramped(key, (F, MT), 0.022 * BINS ** 0.5, (0, 1), top)


def level_of(rng, shape, cuts, least, top_value):
    def one(axis_at, blocks):
        steps = jax.random.uniform(jax.random.fold_in(jax.random.fold_in(rng, 6), axis_at), (blocks,), jnp.float32, least / len(cuts), top_value / len(cuts))
        return jnp.repeat(jnp.exp(steps), shape[axis_at] // blocks).reshape((-1,) + (1,) * (len(shape) - axis_at - 1))

    level = one(*cuts[0])
    for cut in cuts[1:]:
        level = level * one(*cut)
    return level


def noise(stream_key, shape, scale, most, split=(), kind=jnp.bfloat16):
    level = level_of(stream_key, shape, split, -0.22, 0.18) if split else 1.0
    values = jax.random.normal(stream_key, shape, jnp.float32) * scale * level
    return jnp.minimum(jnp.maximum(values, -most), most).astype(kind)


def setup_inputs(seed: int = 0) -> dict:
    arg_keys = jax.random.split(jax.random.key(seed), 23)
    return {
        "bins": draw_bins(jax.random.fold_in(arg_keys[22], 71), 0),
        "species": draw_species(jax.random.fold_in(arg_keys[22], 71), 0),
        "cot_human": draw_cot_human(jax.random.fold_in(arg_keys[22], 71), 0),
        "cot_mouse": draw_cot_mouse(jax.random.fold_in(arg_keys[22], 71), 0),
        "norm_params": draw_norm_params(jax.random.fold_in(arg_keys[22], 71), 0),
        "norm_first": noise(arg_keys[5], (NP,), (0.055 * BINS ** 0.5), 32.0, ((0, 32),), jnp.float32),
        "norm_second": jnp.clip(jnp.exp(math.log(8.192) - 1.3862944 * jax.random.uniform(arg_keys[6], (NP,), jnp.float32) ** level_of(arg_keys[6], (NP,), ((0, 32),), -0.2, 0.2)), 2.048, 8.192),
        "dilated_weight": draw_dilated_weight(jax.random.fold_in(arg_keys[22], 71), 0),
        "dilated_first": draw_dilated_first(jax.random.fold_in(arg_keys[22], 71), 0),
        "dilated_second": jnp.clip(jnp.exp(math.log(2.94912) - 1.3862944 * jax.random.uniform(arg_keys[9], (3, C, B), jnp.float32) ** level_of(arg_keys[9], (3, C, B), ((1, 32),), -0.2, 0.2)), 0.73728, 2.94912),
        "point_weight": draw_point_weight(jax.random.fold_in(arg_keys[22], 71), 0),
        "point_first": draw_point_first(jax.random.fold_in(arg_keys[22], 71), 0),
        "point_second": jnp.clip(jnp.exp(math.log(2.94912) - 1.3862944 * jax.random.uniform(arg_keys[12], (B, C), jnp.float32) ** level_of(arg_keys[12], (B, C), ((1, 32),), -0.2, 0.2)), 0.73728, 2.94912),
        "final_weight": draw_final_weight(jax.random.fold_in(arg_keys[22], 71), 0),
        "final_first": draw_final_first(jax.random.fold_in(arg_keys[22], 71), 0),
        "final_second": jnp.clip(jnp.exp(math.log(2.94912) - 1.3862944 * jax.random.uniform(arg_keys[15], (C, F), jnp.float32) ** level_of(arg_keys[15], (C, F), ((1, 32),), -0.2, 0.2)), 0.73728, 2.94912),
        "human_weight": draw_human_weight(jax.random.fold_in(arg_keys[22], 71), 0),
        "human_first": draw_human_first(jax.random.fold_in(arg_keys[22], 71), 0),
        "human_second": jnp.clip(jnp.exp(math.log(1.31072) - 1.3862944 * jax.random.uniform(arg_keys[18], (F, HT), jnp.float32) ** level_of(arg_keys[18], (F, HT), ((0, 32),), -0.2, 0.2)), 0.32768, 1.31072),
        "mouse_weight": draw_mouse_weight(jax.random.fold_in(arg_keys[22], 71), 0),
        "mouse_first": draw_mouse_first(jax.random.fold_in(arg_keys[22], 71), 0),
        "mouse_second": jnp.clip(jnp.exp(math.log(1.31072) - 1.3862944 * jax.random.uniform(arg_keys[21], (F, MT), jnp.float32) ** level_of(arg_keys[21], (F, MT), ((0, 32),), -0.2, 0.2)), 0.32768, 1.31072),
    }


@jax.custom_vjp
def low(v):
    return lax.optimization_barrier(v.astype(jnp.bfloat16)).astype(jnp.float32)

@jax.custom_vjp
def low_back(v):
    return v

def low_keep(v):
    return (low(v), None)

def low_pass(kept, grad):
    return (grad,)

def back_keep(v):
    return (v, None)

def back_low(kept, grad):
    return (low(grad),)
low.defvjp(low_keep, low_pass)
low_back.defvjp(back_keep, back_low)
bn_eps = 1e-05
beta_first = 0.9
beta_second = 0.999
adam_eps = 1e-06
decay_rate = 0.01
matrix_rate = 0.5
norm_rate = 0.2
highest_precision = lax.Precision.HIGHEST

def batch_norm(values, gain, shift):
    mean_value = lax.optimization_barrier(jnp.mean(values, 0))
    variance = lax.optimization_barrier(jnp.mean(values * values, 0)) - mean_value * mean_value
    return (values - mean_value) * lax.rsqrt(variance + bn_eps) * gain + shift

def dilated_conv(hidden, kernel_weight):
    window_count = hidden.reshape(WINDOWS, WINDOW_BINS, hidden.shape[1])
    padded_input = jnp.pad(window_count, ((0, 0), (DILATION_GAP, DILATION_GAP), (0, 0)))
    running_total = jnp.zeros((WINDOWS, WINDOW_BINS, kernel_weight.shape[2]), jnp.float32)
    for kernel_tap_index in range(3):
        running_total = running_total + jnp.einsum('uxt,tq->uxq', padded_input[:, kernel_tap_index * DILATION_GAP:kernel_tap_index * DILATION_GAP + WINDOW_BINS], kernel_weight[kernel_tap_index], precision=highest_precision)
    return running_total.reshape(BINS, kernel_weight.shape[2])

def forward(values, norm_params, dilated_weight, point_weight, final_weight, human_weight, mouse_weight, human_rows):
    params = low(norm_params)
    gain_one = params[:C]
    shift_one = params[C:2 * C]
    gain_two = params[2 * C:2 * C + B]
    shift_two = params[2 * C + B:]
    first_hidden = low(jax.nn.gelu(batch_norm(values, gain_one, shift_one)))
    middle = low_back(dilated_conv(first_hidden, low(dilated_weight)))
    hidden_two = low(jax.nn.gelu(batch_norm(middle, gain_two, shift_two)))
    branch = low_back(jnp.dot(hidden_two, low(point_weight), precision=highest_precision))
    residual = values + branch
    lifted = low_back(jnp.dot(low(residual), low(final_weight), precision=highest_precision))
    features = low(jax.nn.gelu(lifted))
    human_logits = low_back(jnp.dot(features, low(human_weight), precision=highest_precision))
    mouse_logits = low_back(jnp.dot(features, low(mouse_weight), precision=highest_precision))
    return (jax.nn.softplus(human_logits) * human_rows[:, None], jax.nn.softplus(mouse_logits) * (1.0 - human_rows)[:, None])

def moments(momentum_old, variance_old, gradient):
    momentum = beta_first * momentum_old + (1.0 - beta_first) * gradient
    variance = beta_second * variance_old + (1.0 - beta_second) * gradient * gradient
    direction = momentum / (1.0 - beta_first ** STEP) / (jnp.sqrt(variance / (1.0 - beta_second ** STEP)) + adam_eps)
    return (momentum, variance, direction)

def lamb_matrix(kernel_weight, momentum_old, variance_old, gradient):
    momentum, variance, direction = moments(momentum_old, variance_old, gradient)
    update = direction + decay_rate * kernel_weight
    weight_norm = jnp.sqrt(jnp.sum(kernel_weight * kernel_weight))
    update_norm = jnp.sqrt(jnp.sum(update * update))
    ratio = weight_norm / (update_norm + adam_eps)
    return (momentum, variance, kernel_weight - matrix_rate * ratio * update, jnp.stack([weight_norm, update_norm, ratio]))

def reference(bins, species, cot_human, cot_mouse, norm_params, norm_first, norm_second, dilated_weight, dilated_first, dilated_second, point_weight, point_first, point_second, final_weight, final_first, final_second, human_weight, human_first, human_second, mouse_weight, mouse_first, mouse_second):
    human_rows = (jnp.repeat(species, WINDOW_BINS) == 0).astype(jnp.float32)
    values = bins.astype(jnp.float32)

    def wrapped(values, norm_params, dilated_weight, point_weight, final_weight, human_weight, mouse_weight):
        return forward(values, norm_params, dilated_weight, point_weight, final_weight, human_weight, mouse_weight, human_rows)
    outputs, pullback = jax.vjp(wrapped, values, norm_params, dilated_weight, point_weight, final_weight, human_weight, mouse_weight)
    grads = pullback((cot_human.astype(jnp.float32), cot_mouse.astype(jnp.float32)))
    norm_momentum, norm_variance, norm_direction = moments(norm_first, norm_second, grads[1])
    norm_updated = norm_params - norm_rate * norm_direction
    dilated_momentum, dilated_variance, dilated_updated, dilated_stats = lamb_matrix(dilated_weight, dilated_first, dilated_second, grads[2])
    point_momentum, point_variance, point_updated, point_stats = lamb_matrix(point_weight, point_first, point_second, grads[3])
    final_momentum, final_variance, final_updated, final_stats = lamb_matrix(final_weight, final_first, final_second, grads[4])
    human_momentum, human_variance, human_updated, human_stats = lamb_matrix(human_weight, human_first, human_second, grads[5])
    mouse_momentum, mouse_variance, mouse_updated, mouse_stats = lamb_matrix(mouse_weight, mouse_first, mouse_second, grads[6])
    trust_stats = jnp.stack([dilated_stats, point_stats, final_stats, human_stats, mouse_stats], 1)
    return (outputs[0], outputs[1], grads[0], norm_momentum, norm_variance, norm_updated, dilated_momentum, dilated_variance, dilated_updated, point_momentum, point_variance, point_updated, final_momentum, final_variance, final_updated, human_momentum, human_variance, human_updated, mouse_momentum, mouse_variance, mouse_updated, trust_stats)
```

```python
import jax
import jax.numpy as jnp
from jax import lax
from jax.sharding import PartitionSpec as P

C = 768
B = 384
DILATION_GAP = 57
WINDOW_BINS = 1024
STEP = 10


bn_eps = 1e-05
beta_first = 0.9
beta_second = 0.999
adam_eps = 1e-06
decay_rate = 0.01
matrix_rate = 0.5
norm_rate = 0.2


def extended(cells, sides, width):
    for axis, dim in sides:
        count = lax.axis_size(axis)
        ends = count - 1
        head = lax.slice_in_dim(cells, 0, width, axis=dim)
        tail = lax.slice_in_dim(cells, cells.shape[dim] - width, cells.shape[dim], axis=dim)
        cells = jnp.concatenate(
            [
                lax.ppermute(tail, axis, [(i, (i + 1) % count) for i in range(ends)]),
                cells,
                lax.ppermute(head, axis, [((i + 1) % count, i) for i in range(ends)]),
            ],
            axis=dim,
        )
    return cells


def gelu_back(inputs, gradient):
    unused, pullback = jax.vjp(jax.nn.gelu, inputs)
    return pullback(gradient)[0]


def contracted_rows(left, right):
    return lax.dot_general(
        left, right, (((0,), (0,)), ((), ())), preferred_element_type=jnp.float32
    )


def contract_cols(left, right):
    return lax.dot_general(
        left, right, (((1,), (1,)), ((), ())), preferred_element_type=jnp.float32
    )


def everywhere(vector):
    axes = ("seq", "trk")
    count = lax.axis_size("seq") * lax.axis_size("trk")
    spread = jnp.broadcast_to(vector[None], (count,) + vector.shape)
    return jnp.sum(lax.all_to_all(spread, axes, 0, 0, tiled=True), 0)


def moments(momentum_old, variance_old, gradient):
    momentum = beta_first * momentum_old + (1.0 - beta_first) * gradient
    variance = beta_second * variance_old + (1.0 - beta_second) * gradient * gradient
    direction = (
        momentum
        / (1.0 - beta_first**STEP)
        / (jnp.sqrt(variance / (1.0 - beta_second**STEP)) + adam_eps)
    )
    return (momentum, variance, direction)


def body(
    bins,
    species,
    cot_human,
    cot_mouse,
    norm_params,
    norm_first,
    norm_second,
    dilated_weight,
    dilated_first,
    dilated_second,
    point_weight,
    point_first,
    point_second,
    final_weight,
    final_first,
    final_second,
    human_weight,
    human_first,
    human_second,
    mouse_weight,
    mouse_first,
    mouse_second,
):
    window_rows = bins.shape[0]
    seq_count = lax.axis_size("seq")
    trk_count = lax.axis_size("trk")
    total_rows = window_rows * seq_count * trk_count
    window_len = WINDOW_BINS
    first_row = lax.axis_index(("seq", "trk")) * window_rows
    window_id = first_row // window_len
    human_flag = lax.dynamic_index_in_dim(species, window_id, keepdims=False) == 0
    human_mask = human_flag.astype(jnp.float32)
    devices = seq_count * trk_count
    low = jnp.bfloat16
    flat = jnp.concatenate(
        [
            dilated_weight.astype(low).reshape(-1),
            point_weight.T.astype(low).reshape(-1),
            final_weight.T.astype(low).reshape(-1),
            jnp.pad(norm_params.astype(low), (0, -norm_params.shape[0] % 128)),
        ]
    )
    trunk = lax.all_gather(flat.reshape(-1, 128), ("seq", "trk"), axis=0)
    trunk = trunk.reshape(devices, -1)
    ends = [dilated_weight.size, point_weight.size, final_weight.size]
    ends = [ends[0], ends[0] + ends[1], ends[0] + ends[1] + ends[2]]
    dilated_full = (
        trunk[:, : ends[0]].reshape((devices,) + dilated_weight.shape).transpose(1, 0, 2, 3)
    ).reshape(3, C, B)
    point_full = trunk[:, ends[0] : ends[1]].reshape(C, B).T
    final_full = trunk[:, ends[1] : ends[2]].reshape(-1, C).T
    params = trunk[:, ends[2] : ends[2] + norm_params.shape[0]].reshape(-1).astype(jnp.float32)
    gain_one = params[:C]
    shift_one = params[C : 2 * C]
    gain_two = params[2 * C : 2 * C + B]
    shift_two = params[2 * C + B :]
    values = bins.astype(jnp.float32)
    one_stats = everywhere(jnp.stack([jnp.sum(values, 0), jnp.sum(values * values, 0)]))
    mean_one = one_stats[0] / total_rows
    inverse_one = lax.rsqrt(one_stats[1] / total_rows - mean_one * mean_one + bn_eps)
    normed_one = (values - mean_one) * inverse_one
    affine_one = normed_one * gain_one + shift_one
    first_hidden = jax.nn.gelu(affine_one).astype(jnp.bfloat16)
    tap_positions = first_row - DILATION_GAP + jnp.arange(window_rows + 2 * DILATION_GAP)
    interior_slice = (jnp.floor_divide(tap_positions, window_len) == window_id).astype(
        jnp.bfloat16
    )[:, None]
    padded_input = extended(first_hidden, (("trk", 0),), DILATION_GAP) * interior_slice
    middle = jnp.zeros((window_rows, B), jnp.float32)
    for kernel_tap_index in range(3):
        middle = middle + jnp.dot(
            padded_input[
                kernel_tap_index * DILATION_GAP : kernel_tap_index * DILATION_GAP + window_rows
            ],
            dilated_full[kernel_tap_index],
            preferred_element_type=jnp.float32,
        )
    two_stats = everywhere(jnp.stack([jnp.sum(middle, 0), jnp.sum(middle * middle, 0)]))
    mean_two = two_stats[0] / total_rows
    inverse_two = lax.rsqrt(two_stats[1] / total_rows - mean_two * mean_two + bn_eps)
    normed_two = (middle - mean_two) * inverse_two
    affine_two = normed_two * gain_two + shift_two
    hidden_two = jax.nn.gelu(affine_two).astype(jnp.bfloat16)
    residual = values + jnp.dot(hidden_two, point_full, preferred_element_type=jnp.float32)
    residual_low = residual.astype(jnp.bfloat16)
    lifted = jnp.dot(residual_low, final_full, preferred_element_type=jnp.float32)
    features = jax.nn.gelu(lifted).astype(jnp.bfloat16)
    human_cols = cot_human.shape[1]
    head_low = (human_weight.astype(jnp.bfloat16), mouse_weight.astype(jnp.bfloat16))
    human_pad = human_cols + -human_cols % 128
    heads = jnp.concatenate([jnp.pad(head_low[0], ((0, 0), (0, human_pad - human_cols))), head_low[1]], 1)
    heads = lax.all_gather(heads, ("seq", "trk"), axis=0, tiled=True)
    pieces = (heads[:, :human_cols], heads[:, human_pad:])
    columns = features
    human_logits = jnp.dot(columns, pieces[0], preferred_element_type=jnp.float32)
    mouse_logits = jnp.dot(columns, pieces[1], preferred_element_type=jnp.float32)
    human_output = jax.nn.softplus(human_logits) * human_mask
    mouse_output = jax.nn.softplus(mouse_logits) * (1.0 - human_mask)
    human_slope = (
        cot_human.astype(jnp.float32) * human_mask * jax.nn.sigmoid(human_logits)
    ).astype(jnp.bfloat16)
    mouse_slope = (
        cot_mouse.astype(jnp.float32) * (1.0 - human_mask) * jax.nn.sigmoid(mouse_logits)
    ).astype(jnp.bfloat16)
    joint_slope = jnp.concatenate(
        [jnp.pad(human_slope, ((0, 0), (0, human_pad - human_cols))), mouse_slope], 1
    )
    part = contract_cols(human_slope, pieces[0]) + contract_cols(mouse_slope, pieces[1])
    columns = features
    head_sum = lax.psum_scatter(
        contracted_rows(columns, joint_slope).astype(low), ("seq", "trk"), scatter_dimension=0, tiled=True
    )
    lifted_grad = gelu_back(lifted, part).astype(jnp.bfloat16)
    final_grad = contracted_rows(residual_low, lifted_grad)
    residual_grad = contract_cols(lifted_grad, final_full)
    branch_grad = residual_grad.astype(jnp.bfloat16)
    point_grad = contracted_rows(hidden_two, branch_grad)
    affine_two_grad = gelu_back(affine_two, contract_cols(branch_grad, point_full))
    two_back = everywhere(
        jnp.stack([jnp.sum(affine_two_grad * normed_two, 0), jnp.sum(affine_two_grad, 0)])
    )
    central_gradient = (
        gain_two
        * inverse_two
        * (affine_two_grad - two_back[1] / total_rows - normed_two * two_back[0] / total_rows)
    ).astype(jnp.bfloat16)
    padded_gradient = extended(central_gradient, (("trk", 0),), DILATION_GAP) * interior_slice
    hidden_one_grad = jnp.zeros((window_rows, C), jnp.float32)
    tap_grads = []
    for kernel_tap_index in range(3):
        tap_shift = (2 - kernel_tap_index) * DILATION_GAP
        hidden_one_grad = hidden_one_grad + contract_cols(
            padded_gradient[tap_shift : tap_shift + window_rows], dilated_full[kernel_tap_index]
        )
        tap_grads.append(
            contracted_rows(
                padded_input[
                    kernel_tap_index * DILATION_GAP : kernel_tap_index * DILATION_GAP + window_rows
                ],
                central_gradient,
            )
        )
    dilated_grad = jnp.stack(tap_grads)
    affine_one_grad = gelu_back(affine_one, hidden_one_grad)
    one_back = everywhere(
        jnp.stack([jnp.sum(affine_one_grad * normed_one, 0), jnp.sum(affine_one_grad, 0)])
    )
    input_grad = residual_grad + gain_one * inverse_one * (
        affine_one_grad - one_back[1] / total_rows - normed_one * one_back[0] / total_rows
    )
    norm_full = jnp.concatenate([one_back[0], one_back[1], two_back[0], two_back[1]])
    shard_len = norm_params.shape[0]
    norm_grad = lax.dynamic_slice_in_dim(
        norm_full, lax.axis_index(("seq", "trk")) * shard_len, shard_len
    )
    norm_momentum, norm_variance, norm_direction = moments(norm_first, norm_second, norm_grad)
    norm_updated = norm_params - norm_rate * norm_direction
    flat_grads = jnp.concatenate(
        [
            dilated_grad.astype(low).reshape(3, devices, -1).transpose(1, 0, 2).reshape(devices, -1),
            point_grad.astype(low).T.reshape(devices, -1),
            final_grad.astype(low).T.reshape(devices, -1),
        ],
        1,
    )
    flat_sum = lax.psum_scatter(
        flat_grads.reshape(devices, -1, 128), ("seq", "trk"), scatter_dimension=0, tiled=True
    ).reshape(-1)
    flat_sum = flat_sum.astype(jnp.float32)
    dilated_sum = flat_sum[: ends[0]].reshape(dilated_weight.shape)
    point_sum = flat_sum[ends[0] : ends[1]].reshape(point_weight.shape[::-1]).T
    final_sum = flat_sum[ends[1] : ends[2]].reshape(final_weight.shape[::-1]).T
    head_sum = head_sum.astype(jnp.float32)
    human_sum = head_sum[:, :human_cols]
    mouse_sum = head_sum[:, human_pad:]
    matrices = [
        (dilated_weight, dilated_first, dilated_second, dilated_sum),
        (point_weight, point_first, point_second, point_sum),
        (final_weight, final_first, final_second, final_sum),
        (human_weight, human_first, human_second, human_sum),
        (mouse_weight, mouse_first, mouse_second, mouse_sum),
    ]
    results = []
    weight_squares = []
    update_squares = []
    for kernel_weight, momentum_old, variance_old, gradient in matrices:
        momentum, variance, direction = moments(momentum_old, variance_old, gradient)
        update = direction + decay_rate * kernel_weight
        results.append((momentum, variance, update, kernel_weight))
        weight_squares.append(jnp.sum(kernel_weight * kernel_weight))
        update_squares.append(jnp.sum(update * update))
    square_sums = everywhere(jnp.stack([jnp.stack(weight_squares), jnp.stack(update_squares)]))
    weight_norm = jnp.sqrt(square_sums[0])
    update_norm = jnp.sqrt(square_sums[1])
    ratio = weight_norm / (update_norm + adam_eps)
    updated = [
        results[index][3] - matrix_rate * ratio[index] * results[index][2] for index in range(5)
    ]
    trust_stats = jnp.stack([weight_norm, update_norm, ratio])
    return (
        human_output,
        mouse_output,
        input_grad,
        norm_momentum,
        norm_variance,
        norm_updated,
        results[0][0],
        results[0][1],
        updated[0],
        results[1][0],
        results[1][1],
        updated[1],
        results[2][0],
        results[2][1],
        updated[2],
        results[3][0],
        results[3][1],
        updated[3],
        results[4][0],
        results[4][1],
        updated[4],
        trust_stats,
    )


def solution(mesh):
    in_specs = (
        P(("seq", "trk"), None),
        P(),
        P(("seq", "trk"), None),
        P(("seq", "trk"), None),
        P(("seq", "trk")),
        P(("seq", "trk")),
        P(("seq", "trk")),
        P(None, ("seq", "trk"), None),
        P(None, ("seq", "trk"), None),
        P(None, ("seq", "trk"), None),
        P(None, ("seq", "trk")),
        P(None, ("seq", "trk")),
        P(None, ("seq", "trk")),
        P(None, ("seq", "trk")),
        P(None, ("seq", "trk")),
        P(None, ("seq", "trk")),
        P(("seq", "trk"), None),
        P(("seq", "trk"), None),
        P(("seq", "trk"), None),
        P(("seq", "trk"), None),
        P(("seq", "trk"), None),
        P(("seq", "trk"), None),
    )
    out_specs = (
        P(("seq", "trk"), None),
        P(("seq", "trk"), None),
        P(("seq", "trk"), None),
        P(("seq", "trk")),
        P(("seq", "trk")),
        P(("seq", "trk")),
        P(None, ("seq", "trk"), None),
        P(None, ("seq", "trk"), None),
        P(None, ("seq", "trk"), None),
        P(None, ("seq", "trk")),
        P(None, ("seq", "trk")),
        P(None, ("seq", "trk")),
        P(None, ("seq", "trk")),
        P(None, ("seq", "trk")),
        P(None, ("seq", "trk")),
        P(("seq", "trk"), None),
        P(("seq", "trk"), None),
        P(("seq", "trk"), None),
        P(("seq", "trk"), None),
        P(("seq", "trk"), None),
        P(("seq", "trk"), None),
        P(),
    )
    return jax.shard_map(body, mesh=mesh, in_specs=in_specs, out_specs=out_specs, check_vma=False)
```

```python
import functools

import jax
import jax.numpy as jnp
from jax import lax
from jax.experimental import pallas as pl
from jax.experimental.pallas import tpu as pltpu
from jax.sharding import PartitionSpec as P

C = 768
B = 384
DILATION_GAP = 57
WINDOW_BINS = 1024
STEP = 10


bn_eps = 1e-05
beta_first = 0.9
beta_second = 0.999
adam_eps = 1e-06
decay_rate = 0.01
matrix_rate = 0.5
norm_rate = 0.2


def extended(cells, sides, width):
    for axis, dim in sides:
        count = lax.axis_size(axis)
        ends = count - 1
        head = lax.slice_in_dim(cells, 0, width, axis=dim)
        tail = lax.slice_in_dim(cells, cells.shape[dim] - width, cells.shape[dim], axis=dim)
        cells = jnp.concatenate(
            [
                lax.ppermute(tail, axis, [(i, (i + 1) % count) for i in range(ends)]),
                cells,
                lax.ppermute(head, axis, [((i + 1) % count, i) for i in range(ends)]),
            ],
            axis=dim,
        )
    return cells


def gelu_back(inputs, gradient):
    unused, pullback = jax.vjp(jax.nn.gelu, inputs)
    return pullback(gradient)[0]


def contracted_rows(left, right):
    return lax.dot_general(
        left, right, (((0,), (0,)), ((), ())), preferred_element_type=jnp.float32
    )


def contract_cols(left, right):
    return lax.dot_general(
        left, right, (((1,), (1,)), ((), ())), preferred_element_type=jnp.float32
    )


def everywhere(vector):
    axes = ("seq", "trk")
    count = lax.axis_size("seq") * lax.axis_size("trk")
    spread = jnp.broadcast_to(vector[None], (count,) + vector.shape)
    return jnp.sum(lax.all_to_all(spread, axes, 0, 0, tiled=True), 0)


def partner(cells, axis, mask):
    return lax.ppermute(cells, axis, [(i, i ^ mask) for i in range(lax.axis_size(axis))])


def digits(count):
    found = [(0, 2)]
    shift = 1
    while 1 << shift < count:
        radix = 4 if count >> shift >= 4 else 2
        found.append((shift, radix))
        shift += radix // 2
    return found


def turned(parts, digit):
    bit = 1
    while bit < len(parts):
        flag = digit & bit != 0
        parts = [jnp.where(flag, parts[r ^ bit], parts[r]) for r in range(len(parts))]
        bit *= 2
    return parts


def collected(block):
    cells = block[None]
    steps = [("seq", shift, radix) for shift, radix in reversed(digits(lax.axis_size("seq")))]
    steps += [("trk", shift, radix) for shift, radix in reversed(digits(lax.axis_size("trk")))]
    for axis, shift, radix in steps:
        parts = [cells] + [partner(cells, axis, r << shift) for r in range(1, radix)]
        parts = turned(parts, lax.axis_index(axis) >> shift)
        cells = jnp.stack(parts, 1).reshape((-1,) + block.shape)
    return cells


def summed_digits(total, steps):
    for shift, radix in steps:
        parts = total.reshape((radix, -1) + total.shape[1:])
        total = parts[0]
        sent = [parts[r].astype(jnp.bfloat16) for r in range(1, radix)]
        for r in range(1, radix):
            total = total + partner(sent[r - 1], "seq", r << shift).astype(jnp.float32)
    return total


def relative(cells, axis, digit):
    parts = [lax.index_in_dim(cells, r, axis, keepdims=False) for r in range(cells.shape[axis])]
    return jnp.stack(turned(parts, digit), axis)


def halved(cells, at, axis, shift):
    digit = lax.axis_index(axis) >> shift & 1
    pick = lambda r: lax.dynamic_index_in_dim(cells, digit ^ r, at, keepdims=False)
    got = partner(pick(1).astype(jnp.bfloat16), axis, 1 << shift)
    return pick(0).astype(jnp.float32) + got.astype(jnp.float32)


def scattered_near(cells):
    shape = cells.shape[1:]
    cut = shape[0] // 2
    cells = halved(cells.reshape((-1, 2, 2, 2) + shape), 3, "trk", 0)
    first, second = cells[:, :, :, :cut], cells[:, :, :, cut:]
    first = halved(first, 2, "trk", 1)
    second = halved(second, 1, "seq", 0)
    first = halved(first, 1, "seq", 0)
    second = halved(second, 1, "trk", 1)
    return jnp.concatenate([first, second], 1)


def scattered_far(cells):
    steps = digits(lax.axis_size("seq"))[1:]
    shape = cells.shape[1:]
    cells = cells.reshape(tuple(radix for _, radix in reversed(steps)) + shape)
    for place, (shift, radix) in enumerate(steps):
        cells = relative(cells, len(steps) - 1 - place, lax.axis_index("seq") >> shift)
    cells = cells.transpose(tuple(range(len(steps) - 1, -1, -1)) + (len(steps), len(steps) + 1))
    return summed_digits(cells.reshape((-1,) + shape[1:]), steps)


def relative_rows(features):
    steps = digits(lax.axis_size("seq"))[1:]
    columns = features.shape[1]
    count = len(steps)
    cells = features.reshape(tuple(radix for _, radix in reversed(steps)) + (2, 2, -1, columns))
    for place, (shift, radix) in enumerate(steps):
        cells = relative(cells, count - 1 - place, lax.axis_index("seq") >> shift)
    higher = tuple(range(count - 1, -1, -1))
    along_y = relative(cells, count, lax.axis_index("seq") & 1)
    along_x = relative(cells, count + 1, lax.axis_index("trk") >> 1)
    along_y = along_y.transpose((count,) + higher + (count + 1, count + 2, count + 3))
    along_x = along_x.transpose((count + 1,) + higher + (count, count + 2, count + 3))
    return along_y.reshape(-1, columns), along_x.reshape(-1, columns)


def after(cells, other):
    return cells + (other[(slice(0, 1),) * other.ndim].reshape((1,) * cells.ndim) * 0).astype(cells.dtype)


def sides():
    core = lax.axis_index("trk") & 1
    x_place = lax.axis_index("trk")
    y_place = (lax.axis_index("seq") & 1) * 2 + core
    return (("trk", 2, x_place), ("seq", 1, y_place))


def group_features(along_y, along_x):
    pairs = [(along_y, partner(along_y, "trk", 2)), (along_x, partner(along_x, "seq", 1))]
    return [
        jnp.concatenate([own, got, partner(own, "trk", 1), partner(got, "trk", 1)], 1)
        for own, got in pairs
    ]


def group_columns(slopes):
    kept, given = [], []
    for cells, (axis, mask, place) in zip(slopes, sides()):
        pick = lambda r: lax.dynamic_index_in_dim(cells, place ^ r, 1, keepdims=False)
        got = partner(jnp.stack([pick(2), pick(3)]), axis, mask)
        kept.append(jnp.concatenate([pick(0), got[0]], 2))
        given.append(jnp.concatenate([pick(1), got[1]], 2))
    got = partner(jnp.stack(given), "trk", 1)
    return [jnp.concatenate([kept[k], got[k]], 2) for k in range(2)]


def product(left, right):
    return lax.dot_general(left, right, (((1,), (1,)), ((), ())), preferred_element_type=jnp.float32)


def halved_products(features, columns, part):
    totals = []
    for left, right, (axis, mask, place) in zip(features, columns, sides()):
        cut = left.shape[0] // 2
        other_axis, other_mask = ("seq", 1) if axis == "trk" else ("trk", 2)
        got = partner(product(left[cut:], right[part]).astype(jnp.bfloat16), other_axis, other_mask)
        totals.append(product(left[:cut], right[part]) + got.astype(jnp.float32))
    return jnp.concatenate(totals, 1)


def own_rows(total):
    columns = total.shape[1] // 2
    kept, given = [], []
    for index, (axis, mask, place) in enumerate(sides()):
        cells = total[:, index * columns : (index + 1) * columns].reshape(2, 2, -1, columns)
        digit, core = place >> 1, place & 1
        pick = lambda r: lax.dynamic_index_in_dim(cells, digit ^ r, 0, keepdims=False)
        got = partner(pick(1), axis, mask)
        pair = jnp.stack([jnp.where(digit == 0, pick(0), got), jnp.where(digit == 0, got, pick(0))], 1)
        kept.append(lax.dynamic_index_in_dim(pair, core, 0, keepdims=False))
        given.append(lax.dynamic_index_in_dim(pair, core ^ 1, 0, keepdims=False))
    got = partner(jnp.stack(given), "trk", 1)
    results = []
    for index, (axis, mask, place) in enumerate(sides()):
        core = place & 1
        parts = [
            jnp.where(core == 0, kept[index], got[index]),
            jnp.where(core == 0, got[index], kept[index]),
        ]
        cells = jnp.stack(parts, 1).transpose(2, 0, 1, 3)
        results.append(cells.reshape(cells.shape[0], 4 * columns).astype(jnp.float32))
    return results


def head_kernel(
    human_cols, flag, features, weights, cot_human, cot_mouse, human, mouse, slopes, total
):
    step = pl.program_id(0)
    chunk = slopes.shape[0]
    sub = 256

    @pl.when(step == 0)
    def _():
        total[...] = jnp.zeros_like(total)

    def run(cots, out, first, width):
        parts = []
        for at in range(0, chunk, sub):
            rows = max(min(sub, out.shape[0] - at), 0)
            logits = jnp.dot(
                features[...], weights[:, at : at + sub], preferred_element_type=jnp.float32
            ).T
            small = jnp.exp(-jnp.abs(logits))
            sigmoid = jnp.where(logits >= 0, 1.0, small) / (1.0 + small)
            positive = jnp.maximum(logits, 0.0) + jnp.log1p(small)
            slope = jnp.zeros_like(logits)
            if rows:
                out[at : at + rows, :] = positive[:rows]
                slope = cots[at : at + rows, :].astype(jnp.float32) * sigmoid[:rows]
            if rows and rows < sub:
                slope = jnp.concatenate([slope, jnp.zeros((sub - rows, slope.shape[1]), jnp.float32)])
            column = first + at + lax.broadcasted_iota(jnp.int32, slope.shape, 0)
            slope = jnp.where(column < width, slope, 0.0).astype(jnp.bfloat16)
            slopes[at : at + sub, :] = slope
            parts.append(slope)
        total[...] += jnp.dot(
            weights[...], jnp.concatenate(parts, 0), preferred_element_type=jnp.float32
        )

    @pl.when((step < 3) & (flag[0] != 0))
    def _():
        run(cot_human, human, step * chunk, human_cols)

    @pl.when((step == 3) & (flag[0] == 0))
    def _():
        run(cot_mouse, mouse, 0, cot_mouse.shape[0])

    @pl.when((step < 3) & (flag[0] == 0))
    def _():
        human[...] = jnp.zeros_like(human)
        slopes[...] = jnp.zeros_like(slopes)

    @pl.when((step == 3) & (flag[0] != 0))
    def _():
        mouse[...] = jnp.zeros_like(mouse)
        slopes[...] = jnp.zeros_like(slopes)


def heads_part(flag, features, heads, cot_human, cot_mouse, chunk):
    rows, depth = features.shape
    human_cols, mouse_cols = cot_human.shape[0], cot_mouse.shape[0]
    return pl.pallas_call(
        functools.partial(head_kernel, human_cols),
        grid_spec=pltpu.PrefetchScalarGridSpec(
            num_scalar_prefetch=1,
            grid=(4,),
            in_specs=[
                pl.BlockSpec((rows, depth), lambda i, flag: (0, 0)),
                pl.BlockSpec(
                    (depth, chunk), lambda i, flag: (0, jnp.where(flag[0] != 0, jnp.minimum(i, 2), 3))
                ),
                pl.BlockSpec(
                    (chunk, rows), lambda i, flag: (jnp.where(flag[0] != 0, jnp.minimum(i, 2), 0), 0)
                ),
                pl.BlockSpec((mouse_cols, rows), lambda i, flag: (0, 0)),
            ],
            out_specs=[
                pl.BlockSpec((chunk, rows), lambda i, flag: (jnp.minimum(i, 2), 0)),
                pl.BlockSpec((mouse_cols, rows), lambda i, flag: (0, 0)),
                pl.BlockSpec((chunk, rows), lambda i, flag: (i, 0)),
                pl.BlockSpec((depth, rows), lambda i, flag: (0, 0)),
            ],
        ),
        out_shape=[
            jax.ShapeDtypeStruct((human_cols, rows), jnp.float32),
            jax.ShapeDtypeStruct((mouse_cols, rows), jnp.float32),
            jax.ShapeDtypeStruct((4 * chunk, rows), jnp.bfloat16),
            jax.ShapeDtypeStruct((depth, rows), jnp.float32),
        ],
        compiler_params=pltpu.CompilerParams(vmem_limit_bytes=48 * 2**20),
    )(flag, features, heads, cot_human, cot_mouse)


def moments(momentum_old, variance_old, gradient):
    momentum = beta_first * momentum_old + (1.0 - beta_first) * gradient
    variance = beta_second * variance_old + (1.0 - beta_second) * gradient * gradient
    direction = (
        momentum
        / (1.0 - beta_first**STEP)
        / (jnp.sqrt(variance / (1.0 - beta_second**STEP)) + adam_eps)
    )
    return (momentum, variance, direction)


def body(
    bins,
    species,
    cot_human,
    cot_mouse,
    norm_params,
    norm_first,
    norm_second,
    dilated_weight,
    dilated_first,
    dilated_second,
    point_weight,
    point_first,
    point_second,
    final_weight,
    final_first,
    final_second,
    human_weight,
    human_first,
    human_second,
    mouse_weight,
    mouse_first,
    mouse_second,
):
    window_rows = bins.shape[0]
    seq_count = lax.axis_size("seq")
    trk_count = lax.axis_size("trk")
    total_rows = window_rows * seq_count * trk_count
    window_len = WINDOW_BINS
    first_row = lax.axis_index(("seq", "trk")) * window_rows
    window_id = first_row // window_len
    human_flag = lax.dynamic_index_in_dim(species, window_id, keepdims=False) == 0
    devices = seq_count * trk_count
    low = jnp.bfloat16
    human_cols = cot_human.shape[1]
    mouse_cols = cot_mouse.shape[1]
    chunk = -(-human_cols // 768) * 256
    heads = jnp.concatenate(
        [
            jnp.pad(human_weight.astype(low), ((0, 0), (0, 3 * chunk - human_cols))),
            jnp.pad(mouse_weight.astype(low), ((0, 0), (0, chunk - mouse_cols))),
        ],
        1,
    )
    heads = lax.all_gather(heads, ("seq", "trk"), axis=0, tiled=True)
    own = dilated_weight.shape[1]
    low_params = norm_params.astype(low)
    low_params = jnp.pad(low_params, (0, 8 * B - low_params.shape[0])).reshape(8, B)
    early = jnp.concatenate([dilated_weight.astype(low).reshape(-1, B), low_params])
    final_low = final_weight.T.astype(low)
    late = jnp.concatenate([point_weight.T.astype(low), final_low[:, :B], final_low[:, B:]])
    early = collected(early)
    late = collected(late)
    dilated_full = early[:, : 3 * own].reshape(devices, 3, own, B).transpose(1, 0, 2, 3)
    dilated_full = dilated_full.reshape(3, C, B)
    params = early[:, 3 * own, : norm_params.shape[0]].reshape(-1).astype(jnp.float32)
    point_full = late[:, :own].reshape(C, B)
    final_full = jnp.concatenate(
        [late[:, own : 3 * own].reshape(-1, B), late[:, 3 * own :].reshape(-1, B)], 1
    )
    gain_one = params[:C]
    shift_one = params[C : 2 * C]
    gain_two = params[2 * C : 2 * C + B]
    shift_two = params[2 * C + B :]
    values = bins.astype(jnp.float32)
    one_stats = everywhere(jnp.stack([jnp.sum(values, 0), jnp.sum(values * values, 0)]))
    mean_one = one_stats[0] / total_rows
    inverse_one = lax.rsqrt(one_stats[1] / total_rows - mean_one * mean_one + bn_eps)
    normed_one = (values - mean_one) * inverse_one
    affine_one = normed_one * gain_one + shift_one
    first_hidden = jax.nn.gelu(affine_one).astype(jnp.bfloat16)
    tap_positions = first_row - DILATION_GAP + jnp.arange(window_rows + 2 * DILATION_GAP)
    interior_slice = (jnp.floor_divide(tap_positions, window_len) == window_id).astype(
        jnp.bfloat16
    )[:, None]
    padded_input = extended(first_hidden, (("trk", 0),), DILATION_GAP) * interior_slice
    middle = jnp.zeros((window_rows, B), jnp.float32)
    for kernel_tap_index in range(3):
        middle = middle + jnp.dot(
            padded_input[
                kernel_tap_index * DILATION_GAP : kernel_tap_index * DILATION_GAP + window_rows
            ],
            dilated_full[kernel_tap_index],
            preferred_element_type=jnp.float32,
        )
    two_stats = everywhere(jnp.stack([jnp.sum(middle, 0), jnp.sum(middle * middle, 0)]))
    mean_two = two_stats[0] / total_rows
    inverse_two = lax.rsqrt(two_stats[1] / total_rows - mean_two * mean_two + bn_eps)
    normed_two = (middle - mean_two) * inverse_two
    affine_two = normed_two * gain_two + shift_two
    hidden_two = jax.nn.gelu(affine_two).astype(jnp.bfloat16)
    residual = values + contract_cols(hidden_two, point_full)
    residual_low = residual.astype(jnp.bfloat16)
    lifted = contract_cols(residual_low, final_full)
    features = jax.nn.gelu(lifted).astype(jnp.bfloat16)
    rows_features = group_features(*relative_rows(features.T))
    human_out, mouse_out, slopes, part = heads_part(
        human_flag.astype(jnp.int32).reshape(1), features, heads, cot_human.T, cot_mouse.T, chunk
    )
    slopes = slopes.reshape(2, 2, 4, chunk // 4, window_rows)
    columns = group_columns((slopes[:, 0], slopes[:, 1]))
    early_total = halved_products(rows_features, columns, 0)
    late_total = halved_products(rows_features, columns, 1)
    human_output = human_out.T
    mouse_output = mouse_out.T
    part = part.T
    lifted_grad = gelu_back(lifted, part).astype(jnp.bfloat16)
    final_grad = contracted_rows(lifted_grad, residual_low)
    residual_grad = jnp.dot(lifted_grad, final_full, preferred_element_type=jnp.float32)
    branch_grad = residual_grad.astype(jnp.bfloat16)
    point_grad = contracted_rows(branch_grad, hidden_two)
    affine_two_grad = gelu_back(
        affine_two, jnp.dot(branch_grad, point_full, preferred_element_type=jnp.float32)
    )
    two_back = everywhere(
        jnp.stack([jnp.sum(affine_two_grad * normed_two, 0), jnp.sum(affine_two_grad, 0)])
    )
    central_gradient = (
        gain_two
        * inverse_two
        * (affine_two_grad - two_back[1] / total_rows - normed_two * two_back[0] / total_rows)
    ).astype(jnp.bfloat16)
    padded_gradient = extended(central_gradient, (("trk", 0),), DILATION_GAP) * interior_slice
    hidden_one_grad = jnp.zeros((window_rows, C), jnp.float32)
    tap_grads = []
    for kernel_tap_index in range(3):
        tap_shift = (2 - kernel_tap_index) * DILATION_GAP
        hidden_one_grad = hidden_one_grad + contract_cols(
            padded_gradient[tap_shift : tap_shift + window_rows], dilated_full[kernel_tap_index]
        )
        tap_grads.append(
            contracted_rows(
                padded_input[
                    kernel_tap_index * DILATION_GAP : kernel_tap_index * DILATION_GAP + window_rows
                ],
                central_gradient,
            )
        )
    dilated_grad = jnp.stack(tap_grads)
    affine_one_grad = gelu_back(affine_one, hidden_one_grad)
    one_local = jnp.concatenate(
        [jnp.sum(affine_one_grad * normed_one, 0), jnp.sum(affine_one_grad, 0)]
    )
    final_grad = final_grad.astype(low)
    trunk_grads = jnp.concatenate(
        [
            dilated_grad.astype(low).reshape(3, devices, own, B).transpose(1, 0, 2, 3).reshape(devices, -1, B),
            point_grad.astype(low).reshape(devices, own, B),
            final_grad[:, :B].reshape(devices, -1, B),
            final_grad[:, B:].reshape(devices, -1, B),
        ],
        1,
    )
    trunk_near = scattered_near(trunk_grads)
    higher = digits(seq_count)[1:]
    early_total = summed_digits(early_total, higher).astype(low)
    late_total = summed_digits(after(late_total, trunk_near), higher).astype(low)
    trunk_sum = scattered_far(trunk_near)
    head_early = own_rows(early_total)
    head_late = own_rows(late_total)
    dilated_sum = trunk_sum[: 3 * own].reshape(3, own, B)
    point_sum = trunk_sum[3 * own : 4 * own].T
    final_sum = jnp.concatenate([trunk_sum[4 * own : 6 * own], trunk_sum[6 * own :]], 1).T
    human_sum = jnp.concatenate(head_early + [head_late[0]], 1)[:, :human_cols]
    mouse_sum = head_late[1][:, :mouse_cols]
    matrices = [
        (dilated_weight, dilated_first, dilated_second, dilated_sum),
        (point_weight, point_first, point_second, point_sum),
        (final_weight, final_first, final_second, final_sum),
        (human_weight, human_first, human_second, human_sum),
        (mouse_weight, mouse_first, mouse_second, mouse_sum),
    ]
    results = []
    weight_squares = []
    update_squares = []
    for kernel_weight, momentum_old, variance_old, gradient in matrices:
        momentum, variance, direction = moments(momentum_old, variance_old, gradient)
        update = direction + decay_rate * kernel_weight
        results.append((momentum, variance, update, kernel_weight))
        weight_squares.append(jnp.sum(kernel_weight * kernel_weight))
        update_squares.append(jnp.sum(update * update))
    places = jnp.arange(128)
    squares = jnp.zeros((128,), jnp.float32)
    for index, square in enumerate(weight_squares + update_squares):
        squares = jnp.where(places == index, square, squares)
    last_sums = everywhere(jnp.concatenate([one_local, squares]))
    one_back = last_sums[: 2 * C].reshape(2, C)
    square_sums = last_sums[2 * C : 2 * C + 10].reshape(2, 5)
    input_grad = residual_grad + gain_one * inverse_one * (
        affine_one_grad - one_back[1] / total_rows - normed_one * one_back[0] / total_rows
    )
    norm_full = jnp.concatenate([one_back[0], one_back[1], two_back[0], two_back[1]])
    shard_len = norm_params.shape[0]
    norm_grad = lax.dynamic_slice_in_dim(
        norm_full, lax.axis_index(("seq", "trk")) * shard_len, shard_len
    )
    norm_momentum, norm_variance, norm_direction = moments(norm_first, norm_second, norm_grad)
    norm_updated = norm_params - norm_rate * norm_direction
    weight_norm = jnp.sqrt(square_sums[0])
    update_norm = jnp.sqrt(square_sums[1])
    ratio = weight_norm / (update_norm + adam_eps)
    updated = [
        results[index][3] - matrix_rate * ratio[index] * results[index][2] for index in range(5)
    ]
    trust_stats = jnp.stack([weight_norm, update_norm, ratio])
    return (
        human_output,
        mouse_output,
        input_grad,
        norm_momentum,
        norm_variance,
        norm_updated,
        results[0][0],
        results[0][1],
        updated[0],
        results[1][0],
        results[1][1],
        updated[1],
        results[2][0],
        results[2][1],
        updated[2],
        results[3][0],
        results[3][1],
        updated[3],
        results[4][0],
        results[4][1],
        updated[4],
        trust_stats,
    )


def solution(mesh):
    in_specs = (
        P(("seq", "trk"), None),
        P(),
        P(("seq", "trk"), None),
        P(("seq", "trk"), None),
        P(("seq", "trk")),
        P(("seq", "trk")),
        P(("seq", "trk")),
        P(None, ("seq", "trk"), None),
        P(None, ("seq", "trk"), None),
        P(None, ("seq", "trk"), None),
        P(None, ("seq", "trk")),
        P(None, ("seq", "trk")),
        P(None, ("seq", "trk")),
        P(None, ("seq", "trk")),
        P(None, ("seq", "trk")),
        P(None, ("seq", "trk")),
        P(("seq", "trk"), None),
        P(("seq", "trk"), None),
        P(("seq", "trk"), None),
        P(("seq", "trk"), None),
        P(("seq", "trk"), None),
        P(("seq", "trk"), None),
    )
    out_specs = (
        P(("seq", "trk"), None),
        P(("seq", "trk"), None),
        P(("seq", "trk"), None),
        P(("seq", "trk")),
        P(("seq", "trk")),
        P(("seq", "trk")),
        P(None, ("seq", "trk"), None),
        P(None, ("seq", "trk"), None),
        P(None, ("seq", "trk"), None),
        P(None, ("seq", "trk")),
        P(None, ("seq", "trk")),
        P(None, ("seq", "trk")),
        P(None, ("seq", "trk")),
        P(None, ("seq", "trk")),
        P(None, ("seq", "trk")),
        P(("seq", "trk"), None),
        P(("seq", "trk"), None),
        P(("seq", "trk"), None),
        P(("seq", "trk"), None),
        P(("seq", "trk"), None),
        P(("seq", "trk"), None),
        P(),
    )
    return jax.shard_map(body, mesh=mesh, in_specs=in_specs, out_specs=out_specs, check_vma=False)
```

```python
import functools

import jax
import jax.numpy as jnp
from jax import lax
from jax.experimental import pallas as pl
from jax.experimental.pallas import tpu as pltpu
from jax.sharding import PartitionSpec as P

C = 768
B = 384
DILATION_GAP = 57
WINDOW_BINS = 1024
STEP = 10


bn_eps = 1e-05
beta_first = 0.9
beta_second = 0.999
adam_eps = 1e-06
decay_rate = 0.01
matrix_rate = 0.5
norm_rate = 0.2


def extended(cells, sides, width):
    for axis, dim in sides:
        count = lax.axis_size(axis)
        ends = count - 1
        head = lax.slice_in_dim(cells, 0, width, axis=dim)
        tail = lax.slice_in_dim(cells, cells.shape[dim] - width, cells.shape[dim], axis=dim)
        cells = jnp.concatenate(
            [
                lax.ppermute(tail, axis, [(i, (i + 1) % count) for i in range(ends)]),
                cells,
                lax.ppermute(head, axis, [((i + 1) % count, i) for i in range(ends)]),
            ],
            axis=dim,
        )
    return cells


def gelu_back(inputs, gradient):
    unused, pullback = jax.vjp(jax.nn.gelu, inputs)
    return pullback(gradient)[0]


def contracted_rows(left, right):
    return lax.dot_general(
        left, right, (((0,), (0,)), ((), ())), preferred_element_type=jnp.float32
    )


def contract_cols(left, right):
    return lax.dot_general(
        left, right, (((1,), (1,)), ((), ())), preferred_element_type=jnp.float32
    )


def everywhere(vector):
    axes = ("seq", "trk")
    count = lax.axis_size("seq") * lax.axis_size("trk")
    spread = jnp.broadcast_to(vector[None], (count,) + vector.shape)
    return jnp.sum(lax.all_to_all(spread, axes, 0, 0, tiled=True), 0)


def partner(cells, axis, mask):
    return lax.ppermute(cells, axis, [(i, i ^ mask) for i in range(lax.axis_size(axis))])


def digits(count):
    found = [(0, 2)]
    shift = 1
    while 1 << shift < count:
        radix = 4 if count >> shift >= 4 else 2
        found.append((shift, radix))
        shift += radix // 2
    return found


def turned(parts, digit):
    bit = 1
    while bit < len(parts):
        flag = digit & bit != 0
        parts = [jnp.where(flag, parts[r ^ bit], parts[r]) for r in range(len(parts))]
        bit *= 2
    return parts


def collected(block, awaited=None):
    cells = block[None]
    steps = [("seq", shift, radix) for shift, radix in reversed(digits(lax.axis_size("seq")))]
    steps += [("trk", 1, 2), ("trk", 0, 2)]
    for axis, shift, radix in steps:
        if awaited is not None and (axis, shift) == ("trk", 1):
            cells = after(cells, awaited)
        parts = [cells] + [partner(cells, axis, r << shift) for r in range(1, radix)]
        parts = turned(parts, lax.axis_index(axis) >> shift)
        cells = jnp.stack(parts, 1).reshape((-1,) + block.shape)
    return cells


def begun_digits(total, steps):
    radix = steps[0][1]
    parts = total.reshape((radix, -1) + total.shape[1:])
    return parts[0].astype(jnp.float32), [parts[r].astype(jnp.bfloat16) for r in range(1, radix)]


def ended_digits(begun, steps, awaited=()):
    total, sent = begun
    for place, (shift, radix) in enumerate(steps):
        if place:
            total, sent = begun_digits(total, steps[place:])
        for r in range(1, radix):
            got = partner(sent[r - 1], "seq", r << shift)
            for other in awaited:
                got = after(got, other)
            total = total + got.astype(jnp.float32)
    return total


def relative(cells, axis, digit):
    parts = [lax.index_in_dim(cells, r, axis, keepdims=False) for r in range(cells.shape[axis])]
    return jnp.stack(turned(parts, digit), axis)


def split(cells, at, axis, shift):
    digit = lax.axis_index(axis) >> shift & 1
    pick = lambda r: lax.dynamic_index_in_dim(cells, digit ^ r, at, keepdims=False)
    return pick(0).astype(jnp.float32), pick(1).astype(jnp.bfloat16)


def joined(kept, sent, axis, shift, awaited=None):
    got = partner(sent, axis, 1 << shift)
    if awaited is not None:
        got = after(got, awaited)
    return kept + got.astype(jnp.float32)


def relative_blocks(cells):
    steps = digits(lax.axis_size("seq"))[1:]
    shape = cells.shape[1:]
    cells = cells.reshape(tuple(radix for _, radix in reversed(steps)) + shape)
    for place, (shift, radix) in enumerate(steps):
        cells = relative(cells, len(steps) - 1 - place, lax.axis_index("seq") >> shift)
    cells = cells.transpose(tuple(range(len(steps) - 1, -1, -1)) + (len(steps), len(steps) + 1))
    return cells.reshape((-1,) + shape[1:])


def relative_rows(features):
    steps = digits(lax.axis_size("seq"))
    columns = features.shape[1]
    count = len(steps)
    cells = features.reshape(tuple(radix for _, radix in reversed(steps)) + (-1, columns))
    for place, (shift, radix) in enumerate(steps):
        cells = relative(cells, count - 1 - place, lax.axis_index("seq") >> shift)
    cells = cells.transpose(tuple(range(count - 1, -1, -1)) + (count, count + 1))
    return cells.reshape(-1, columns)


def after(cells, other):
    return cells + (other[(slice(0, 1),) * other.ndim].reshape((1,) * cells.ndim) * 0).astype(cells.dtype)


def window_exchanged(cells, awaited=None):
    sent = cells[2:]
    got = partner(sent if awaited is None else after(sent, awaited), "trk", 2)
    sibling = partner(jnp.stack([cells[1], got[1]]), "trk", 1)
    return [cells[0], sibling[0], got[0], sibling[1]]


def by_relation(cells):
    me = lax.axis_index("trk")
    return jnp.stack([lax.dynamic_index_in_dim(cells, me ^ r, 0, keepdims=False) for r in range(4)])


def weights_kernel(quarter, me, human, mouse, out, wide, small):
    wide[:, -128:] = jnp.zeros_like(wide[:, -128:])
    small[:, -256:] = jnp.zeros_like(small[:, -256:])
    wide[:, : human.shape[1]] = human[...]
    small[:, : mouse.shape[1]] = mouse[...]
    for at in range(4):
        cells = jnp.concatenate(
            [
                wide[:, 2 * at * quarter : 2 * (at + 1) * quarter],
                wide[:, (8 + at) * quarter : (9 + at) * quarter],
                small[:, at * quarter : (at + 1) * quarter],
            ],
            1,
        )
        out[me[0] ^ at] = cells.astype(jnp.bfloat16)


def window_weights(human, mouse, quarter):
    rows = human.shape[0]
    full = lambda cells: pl.BlockSpec(cells.shape, lambda i, me: (0, 0))
    shape = (4, rows, 4 * quarter)
    return pl.pallas_call(
        functools.partial(weights_kernel, quarter),
        grid_spec=pltpu.PrefetchScalarGridSpec(
            num_scalar_prefetch=1,
            grid=(1,),
            in_specs=[full(human), full(mouse)],
            out_specs=pl.BlockSpec(shape, lambda i, me: (0, 0, 0)),
            scratch_shapes=[
                pltpu.VMEM((rows, 12 * quarter), jnp.float32),
                pltpu.VMEM((rows, 4 * quarter), jnp.float32),
            ],
        ),
        out_shape=jax.ShapeDtypeStruct(shape, jnp.bfloat16),
        compiler_params=pltpu.CompilerParams(vmem_limit_bytes=24 * 2**20),
    )(lax.axis_index("trk").astype(jnp.int32).reshape(1), human, mouse)


def cots_kernel(human_cols, mouse_cols, scalars, first, last, mouse, out):
    at = pl.program_id(0)
    quarter = last.shape[0]
    row = at * quarter + lax.broadcasted_iota(jnp.int32, last.shape, 0)

    @pl.when(scalars[1] != 0)
    def _():
        out[0, : 2 * quarter] = first[...]
        cells = jnp.where(row < human_cols - 8 * quarter, last[...].astype(jnp.float32), 0.0)
        out[0, 2 * quarter :] = cells.astype(jnp.bfloat16)

    @pl.when(scalars[1] == 0)
    def _():
        out[0, : 2 * quarter] = jnp.zeros_like(first)
        cells = jnp.where(row < mouse_cols, mouse[...].astype(jnp.float32), 0.0)
        out[0, 2 * quarter :] = cells.astype(jnp.bfloat16)


def window_cots(human_flag, human, mouse, quarter):
    bins = human.shape[1]
    scalars = jnp.stack([lax.axis_index("trk"), human_flag]).astype(jnp.int32)
    return pl.pallas_call(
        functools.partial(cots_kernel, human.shape[0], mouse.shape[0]),
        grid_spec=pltpu.PrefetchScalarGridSpec(
            num_scalar_prefetch=1,
            grid=(4,),
            in_specs=[
                pl.BlockSpec((2 * quarter, bins), lambda i, scalars: (i, 0)),
                pl.BlockSpec((quarter, bins), lambda i, scalars: (8 + i, 0)),
                pl.BlockSpec((quarter, bins), lambda i, scalars: (i, 0)),
            ],
            out_specs=pl.BlockSpec((1, 3 * quarter, bins), lambda i, scalars: (scalars[0] ^ i, 0, 0)),
        ),
        out_shape=jax.ShapeDtypeStruct((4, 3 * quarter, bins), jnp.bfloat16),
        compiler_params=pltpu.CompilerParams(vmem_limit_bytes=24 * 2**20),
    )(scalars, human, human, mouse)


def window_bins(cells):
    got = partner(cells, "trk", 2)
    return jnp.concatenate([cells, got, partner(cells, "trk", 1), partner(got, "trk", 1)], 1)


def window_summed(cells):
    half = cells.shape[1] // 2
    quarter = half // 2
    kept = cells[:, :half].astype(jnp.float32)
    kept = kept + partner(cells[:, half:], "trk", 1).astype(jnp.float32)
    sent = kept[:, quarter:].astype(jnp.bfloat16)
    return kept[:, :quarter] + partner(sent, "trk", 2).astype(jnp.float32)


def window_returned(cells, awaited, arrival_awaited):
    half = cells.shape[1] // 2
    quarter = half // 2
    sibling = partner(cells[:, half:], "trk", 1)
    mine = [cells[:, :quarter], sibling[:, :quarter]]
    sent = jnp.stack([cells[:, quarter:half], sibling[:, quarter:]])
    got = after(partner(after(sent, awaited), "trk", 2), arrival_awaited)
    return turned(mine + [got[0], got[1]], lax.axis_index("trk"))


def product(left, right):
    return lax.dot_general(left, right, (((1,), (1,)), ((), ())), preferred_element_type=jnp.float32)


def own_rows(total):
    parts = window_exchanged(by_relation(total.reshape(4, -1, total.shape[1])))
    return turned(parts, lax.axis_index("trk"))


def head_kernel(flag, features, weights, cots, out_first, out_last, total, gradient):
    columns = out_last.shape[0]
    wide = -(-columns // 128) * 128
    human = flag[0] != 0

    def run(first, count, cotangents):
        logits = lax.dot_general(
            weights[:, first : first + count],
            features[...],
            (((0,), (0,)), ((), ())),
            preferred_element_type=jnp.float32,
        )
        small = jnp.exp(-jnp.abs(logits))
        sigmoid = jnp.where(logits >= 0, 1.0, small) / (1.0 + small)
        predicted = (jnp.maximum(logits, 0.0) + jnp.log1p(small)).astype(jnp.bfloat16)
        return predicted, (cotangents.astype(jnp.float32) * sigmoid).astype(jnp.bfloat16)

    def back(first, slopes):
        last = first + slopes.shape[0]
        total[...] = jnp.dot(
            weights[:, first:last], slopes, preferred_element_type=jnp.float32
        ).astype(jnp.bfloat16)
        gradient[:, first:last] = product(features[...], slopes).astype(jnp.bfloat16)
        if first:
            gradient[:, :first] = jnp.zeros_like(gradient[:, :first])
        if last < gradient.shape[1]:
            gradient[:, last:] = jnp.zeros_like(gradient[:, last:])

    gap = jnp.zeros((wide - columns, cots.shape[1]), cots.dtype)

    @pl.when(human)
    def _():
        predicted, first = run(0, 2 * columns, cots[: 2 * columns, :])
        out_first[...] = predicted
        predicted, last = run(2 * columns, wide, jnp.concatenate([cots[2 * columns :, :], gap], 0))
        out_last[...] = predicted[:columns]
        back(0, jnp.concatenate([first, last], 0))

    @pl.when(jnp.logical_not(human))
    def _():
        start = 4 * columns - wide
        predicted, last = run(start, wide, jnp.concatenate([gap, cots[2 * columns :, :]], 0))
        out_first[...] = jnp.zeros_like(out_first)
        out_last[...] = predicted[wide - columns :]
        back(start, last)


def heads_part(flag, features, heads, cots):
    depth, bins = features.shape
    columns = cots.shape[0] // 3
    full = lambda shape: pl.BlockSpec(shape, lambda i, flag: (0, 0))
    shapes = [(2 * columns, bins), (columns, bins), (depth, bins), (depth, 4 * columns)]
    return pl.pallas_call(
        head_kernel,
        grid_spec=pltpu.PrefetchScalarGridSpec(
            num_scalar_prefetch=1,
            grid=(1,),
            in_specs=[full(features.shape), full(heads.shape), full(cots.shape)],
            out_specs=[full(shape) for shape in shapes],
        ),
        out_shape=[jax.ShapeDtypeStruct(shape, jnp.bfloat16) for shape in shapes],
        compiler_params=pltpu.CompilerParams(vmem_limit_bytes=60 * 2**20),
    )(flag, features, heads, cots)


def lanes(cells):
    sums = jnp.sum(cells, tuple(range(cells.ndim - 1)))
    return jnp.sum(jnp.pad(sums, (0, -sums.shape[0] % 128)).reshape(-1, 128), 0)


def moments(momentum_old, variance_old, gradient):
    momentum = beta_first * momentum_old + (1.0 - beta_first) * gradient
    variance = beta_second * variance_old + (1.0 - beta_second) * gradient * gradient
    direction = (
        momentum
        / (1.0 - beta_first**STEP)
        / (jnp.sqrt(variance / (1.0 - beta_second**STEP)) + adam_eps)
    )
    return (momentum, variance, direction)


def body(
    bins,
    species,
    cot_human,
    cot_mouse,
    norm_params,
    norm_first,
    norm_second,
    dilated_weight,
    dilated_first,
    dilated_second,
    point_weight,
    point_first,
    point_second,
    final_weight,
    final_first,
    final_second,
    human_weight,
    human_first,
    human_second,
    mouse_weight,
    mouse_first,
    mouse_second,
):
    window_rows = bins.shape[0]
    seq_count = lax.axis_size("seq")
    trk_count = lax.axis_size("trk")
    total_rows = window_rows * seq_count * trk_count
    window_len = WINDOW_BINS
    first_row = lax.axis_index(("seq", "trk")) * window_rows
    window_id = first_row // window_len
    human_flag = lax.dynamic_index_in_dim(species, window_id, keepdims=False) == 0
    devices = seq_count * trk_count
    low = jnp.bfloat16
    human_cols = cot_human.shape[1]
    mouse_cols = cot_mouse.shape[1]
    quarter = -(-human_cols // 768) * 64
    chunk = 4 * quarter
    heads = window_exchanged(window_weights(human_weight, mouse_weight, quarter))
    heads_arrived = heads[2]
    heads_window = jnp.concatenate(turned(heads, lax.axis_index("trk")))
    heads = lax.all_gather(heads_window, "seq", axis=0, tiled=True)
    cots = window_cots(human_flag, cot_human.T, cot_mouse.T, quarter)
    own = dilated_weight.shape[1]
    low_params = norm_params.astype(low)
    low_params = jnp.pad(low_params, (0, 8 * B - low_params.shape[0])).reshape(8, B)
    early = jnp.concatenate([dilated_weight.astype(low).reshape(-1, B), low_params])
    final_low = final_weight.T.astype(low)
    late = jnp.concatenate([point_weight.T.astype(low), final_low[:, :B], final_low[:, B:]])
    early = collected(early)
    dilated_full = early[:, : 3 * own].reshape(devices, 3, own, B).transpose(1, 0, 2, 3)
    dilated_full = dilated_full.reshape(3, C, B)
    params = early[:, 3 * own, : norm_params.shape[0]].reshape(-1).astype(jnp.float32)
    gain_one = params[:C]
    shift_one = params[C : 2 * C]
    gain_two = params[2 * C : 2 * C + B]
    shift_two = params[2 * C + B :]
    values = bins.astype(jnp.float32)
    one_stats = everywhere(jnp.stack([jnp.sum(values, 0), jnp.sum(values * values, 0)]))
    mean_one = one_stats[0] / total_rows
    inverse_one = lax.rsqrt(one_stats[1] / total_rows - mean_one * mean_one + bn_eps)
    normed_one = (values - mean_one) * inverse_one
    affine_one = normed_one * gain_one + shift_one
    first_hidden = jax.nn.gelu(affine_one).astype(jnp.bfloat16)
    tap_positions = first_row - DILATION_GAP + jnp.arange(window_rows + 2 * DILATION_GAP)
    interior_slice = (jnp.floor_divide(tap_positions, window_len) == window_id).astype(
        jnp.bfloat16
    )[:, None]
    padded_input = extended(first_hidden, (("trk", 0),), DILATION_GAP) * interior_slice
    middle = jnp.zeros((window_rows, B), jnp.float32)
    for kernel_tap_index in range(3):
        middle = middle + jnp.dot(
            padded_input[
                kernel_tap_index * DILATION_GAP : kernel_tap_index * DILATION_GAP + window_rows
            ],
            dilated_full[kernel_tap_index],
            preferred_element_type=jnp.float32,
        )
    two_local = jnp.stack([jnp.sum(middle, 0), jnp.sum(middle * middle, 0)])
    two_stats = everywhere(two_local)
    late = collected(after(late, heads_arrived), two_local)
    point_full = late[:, :own].reshape(C, B)
    final_full = jnp.concatenate(
        [late[:, own : 3 * own].reshape(-1, B), late[:, 3 * own :].reshape(-1, B)], 1
    )
    cots = window_exchanged(cots, two_stats)
    cots = jnp.concatenate([cots[0], cots[2], cots[1], cots[3]], 1)
    mean_two = two_stats[0] / total_rows
    inverse_two = lax.rsqrt(two_stats[1] / total_rows - mean_two * mean_two + bn_eps)
    normed_two = (middle - mean_two) * inverse_two
    affine_two = normed_two * gain_two + shift_two
    hidden_two = jax.nn.gelu(affine_two).astype(jnp.bfloat16)
    residual = values + contract_cols(hidden_two, point_full)
    residual_low = residual.astype(jnp.bfloat16)
    lifted = contract_cols(residual_low, final_full)
    features = jax.nn.gelu(lifted).astype(jnp.bfloat16)
    bins_features = window_bins(features.T)
    first_out, last_out, part, head_grads = heads_part(
        human_flag.astype(jnp.int32).reshape(1), bins_features, heads, cots
    )
    head_sum = lax.psum_scatter(head_grads, "seq", scatter_dimension=0, tiled=True)
    part = window_summed(part)
    part = part.T
    lifted_grad = gelu_back(lifted, part).astype(jnp.bfloat16)
    final_grad = contracted_rows(lifted_grad, residual_low)
    residual_grad = jnp.dot(lifted_grad, final_full, preferred_element_type=jnp.float32)
    branch_grad = residual_grad.astype(jnp.bfloat16)
    point_grad = contracted_rows(branch_grad, hidden_two)
    affine_two_grad = gelu_back(
        affine_two, jnp.dot(branch_grad, point_full, preferred_element_type=jnp.float32)
    )
    two_back = everywhere(
        jnp.stack([jnp.sum(affine_two_grad * normed_two, 0), jnp.sum(affine_two_grad, 0)])
    )
    higher = digits(seq_count)[1:]
    central_gradient = (
        gain_two
        * inverse_two
        * (affine_two_grad - two_back[1] / total_rows - normed_two * two_back[0] / total_rows)
    ).astype(jnp.bfloat16)
    padded_gradient = extended(central_gradient, (("trk", 0),), DILATION_GAP) * interior_slice
    hidden_one_grad = jnp.zeros((window_rows, C), jnp.float32)
    tap_grads = []
    for kernel_tap_index in range(3):
        tap_shift = (2 - kernel_tap_index) * DILATION_GAP
        hidden_one_grad = hidden_one_grad + contract_cols(
            padded_gradient[tap_shift : tap_shift + window_rows], dilated_full[kernel_tap_index]
        )
        tap_grads.append(
            contracted_rows(
                padded_input[
                    kernel_tap_index * DILATION_GAP : kernel_tap_index * DILATION_GAP + window_rows
                ],
                central_gradient,
            )
        )
    dilated_grad = jnp.stack(tap_grads)
    affine_one_grad = gelu_back(affine_one, hidden_one_grad)
    one_local = jnp.concatenate(
        [jnp.sum(affine_one_grad * normed_one, 0), jnp.sum(affine_one_grad, 0)]
    )
    final_grad = final_grad.astype(low)
    trunk_grads = jnp.concatenate(
        [
            dilated_grad.astype(low).reshape(3, devices, own, B).transpose(1, 0, 2, 3).reshape(devices, -1, B),
            point_grad.astype(low).reshape(devices, own, B),
            final_grad[:, :B].reshape(devices, -1, B),
            final_grad[:, B:].reshape(devices, -1, B),
        ],
        1,
    )
    trunk_grads = trunk_grads.reshape((-1, 2, 2, 2) + trunk_grads.shape[1:])
    core = joined(*split(trunk_grads, 3, "trk", 0), "trk", 0)
    half = core.shape[3] // 2
    first, first_sent = split(core[:, :, :, :half], 2, "trk", 1)
    second, second_sent = split(core[:, :, :, half:], 1, "seq", 0)
    first = joined(first, first_sent, "trk", 1)
    second = joined(second, second_sent, "seq", 0)
    first, first_sent = split(first, 1, "seq", 0)
    second, second_sent = split(second, 1, "trk", 1)
    predicted = window_returned(jnp.concatenate([first_out, last_out]), first_sent, head_sum)
    trunk_near = jnp.concatenate(
        [joined(first, first_sent, "seq", 0), joined(second, second_sent, "trk", 1)], 1
    )
    trunk_begun = begun_digits(relative_blocks(trunk_near), higher)
    trunk_sum = ended_digits(trunk_begun, higher)
    head_rows = own_rows(head_sum)
    early_rows = [cells[:, : 2 * quarter] for cells in head_rows]
    late_rows = [cells[:, 2 * quarter :] for cells in head_rows]
    human_rows = human_flag.astype(jnp.float32)
    human_output = jnp.concatenate(
        [cells[: 2 * quarter] for cells in predicted] + [cells[2 * quarter :] for cells in predicted]
    )
    human_output = (human_output[:human_cols].astype(jnp.float32) * human_rows).T
    mouse_output = jnp.concatenate([cells[2 * quarter :] for cells in predicted])
    mouse_output = (mouse_output[:mouse_cols].astype(jnp.float32) * (1.0 - human_rows)).T
    dilated_sum = trunk_sum[: 3 * own].reshape(3, own, B)
    point_sum = trunk_sum[3 * own : 4 * own].T
    final_sum = jnp.concatenate([trunk_sum[4 * own : 6 * own], trunk_sum[6 * own :]], 1).T
    human_sum = jnp.concatenate(early_rows + [cells[:, :quarter] for cells in late_rows], 1)
    human_sum = human_sum[:, :human_cols].astype(jnp.float32)
    mouse_sum = jnp.concatenate([cells[:, quarter:] for cells in late_rows], 1)
    mouse_sum = mouse_sum[:, :mouse_cols].astype(jnp.float32)
    matrices = [
        (dilated_weight, dilated_first, dilated_second, dilated_sum),
        (point_weight, point_first, point_second, point_sum),
        (final_weight, final_first, final_second, final_sum),
        (human_weight, human_first, human_second, human_sum),
        (mouse_weight, mouse_first, mouse_second, mouse_sum),
    ]
    results = []
    weight_squares = []
    update_squares = []
    for kernel_weight, momentum_old, variance_old, gradient in matrices:
        momentum, variance, direction = moments(momentum_old, variance_old, gradient)
        update = direction + decay_rate * kernel_weight
        results.append((momentum, variance, update, kernel_weight))
        tall = kernel_weight.shape[0] > kernel_weight.shape[1] and kernel_weight.ndim == 2
        weight_squares.append(lanes((kernel_weight * kernel_weight).T if tall else kernel_weight * kernel_weight))
        update_squares.append(lanes((update * update).T if tall else update * update))
    last_sums = everywhere(jnp.concatenate([one_local.reshape(-1, 128)] + [jnp.stack(weight_squares + update_squares)]))
    one_back = last_sums[: 2 * C // 128].reshape(2, C)
    square_sums = jnp.sum(last_sums[2 * C // 128 :], 1).reshape(2, 5)
    input_grad = residual_grad + gain_one * inverse_one * (
        affine_one_grad - one_back[1] / total_rows - normed_one * one_back[0] / total_rows
    )
    norm_full = jnp.concatenate([one_back[0], one_back[1], two_back[0], two_back[1]])
    shard_len = norm_params.shape[0]
    norm_grad = lax.dynamic_slice_in_dim(
        norm_full, lax.axis_index(("seq", "trk")) * shard_len, shard_len
    )
    norm_momentum, norm_variance, norm_direction = moments(norm_first, norm_second, norm_grad)
    norm_updated = norm_params - norm_rate * norm_direction
    weight_norm = jnp.sqrt(square_sums[0])
    update_norm = jnp.sqrt(square_sums[1])
    ratio = weight_norm / (update_norm + adam_eps)
    updated = [
        results[index][3] - matrix_rate * ratio[index] * results[index][2] for index in range(5)
    ]
    trust_stats = jnp.stack([weight_norm, update_norm, ratio])
    return (
        human_output,
        mouse_output,
        input_grad,
        norm_momentum,
        norm_variance,
        norm_updated,
        results[0][0],
        results[0][1],
        updated[0],
        results[1][0],
        results[1][1],
        updated[1],
        results[2][0],
        results[2][1],
        updated[2],
        results[3][0],
        results[3][1],
        updated[3],
        results[4][0],
        results[4][1],
        updated[4],
        trust_stats,
    )


def solution(mesh):
    in_specs = (
        P(("seq", "trk"), None),
        P(),
        P(("seq", "trk"), None),
        P(("seq", "trk"), None),
        P(("seq", "trk")),
        P(("seq", "trk")),
        P(("seq", "trk")),
        P(None, ("seq", "trk"), None),
        P(None, ("seq", "trk"), None),
        P(None, ("seq", "trk"), None),
        P(None, ("seq", "trk")),
        P(None, ("seq", "trk")),
        P(None, ("seq", "trk")),
        P(None, ("seq", "trk")),
        P(None, ("seq", "trk")),
        P(None, ("seq", "trk")),
        P(("seq", "trk"), None),
        P(("seq", "trk"), None),
        P(("seq", "trk"), None),
        P(("seq", "trk"), None),
        P(("seq", "trk"), None),
        P(("seq", "trk"), None),
    )
    out_specs = (
        P(("seq", "trk"), None),
        P(("seq", "trk"), None),
        P(("seq", "trk"), None),
        P(("seq", "trk")),
        P(("seq", "trk")),
        P(("seq", "trk")),
        P(None, ("seq", "trk"), None),
        P(None, ("seq", "trk"), None),
        P(None, ("seq", "trk"), None),
        P(None, ("seq", "trk")),
        P(None, ("seq", "trk")),
        P(None, ("seq", "trk")),
        P(None, ("seq", "trk")),
        P(None, ("seq", "trk")),
        P(None, ("seq", "trk")),
        P(("seq", "trk"), None),
        P(("seq", "trk"), None),
        P(("seq", "trk"), None),
        P(("seq", "trk"), None),
        P(("seq", "trk"), None),
        P(("seq", "trk"), None),
        P(),
    )
    return jax.shard_map(body, mesh=mesh, in_specs=in_specs, out_specs=out_specs, check_vma=False)
```

```python
import functools

import jax
import jax.numpy as jnp
from jax import lax
from jax.experimental import pallas as pl
from jax.experimental.pallas import tpu as pltpu
from jax.sharding import PartitionSpec as P

C = 768
B = 384
DILATION_GAP = 57
WINDOW_BINS = 1024
STEP = 10


bn_eps = 1e-05
beta_first = 0.9
beta_second = 0.999
adam_eps = 1e-06
decay_rate = 0.01
matrix_rate = 0.5
norm_rate = 0.2


def extended(cells, sides, width):
    for axis, dim in sides:
        count = lax.axis_size(axis)
        ends = count - 1
        head = lax.slice_in_dim(cells, 0, width, axis=dim)
        tail = lax.slice_in_dim(cells, cells.shape[dim] - width, cells.shape[dim], axis=dim)
        cells = jnp.concatenate(
            [
                lax.ppermute(tail, axis, [(i, (i + 1) % count) for i in range(ends)]),
                cells,
                lax.ppermute(head, axis, [((i + 1) % count, i) for i in range(ends)]),
            ],
            axis=dim,
        )
    return cells


def gelu_back(inputs, gradient):
    unused, pullback = jax.vjp(jax.nn.gelu, inputs)
    return pullback(gradient)[0]


def contracted_rows(left, right):
    return lax.dot_general(
        left, right, (((0,), (0,)), ((), ())), preferred_element_type=jnp.float32
    )


def contract_cols(left, right):
    return lax.dot_general(
        left, right, (((1,), (1,)), ((), ())), preferred_element_type=jnp.float32
    )


def everywhere(vector):
    axes = ("seq", "trk")
    count = lax.axis_size("seq") * lax.axis_size("trk")
    spread = jnp.broadcast_to(vector[None], (count,) + vector.shape)
    return jnp.sum(lax.all_to_all(spread, axes, 0, 0, tiled=True), 0)


def partner(cells, axis, mask):
    return lax.ppermute(cells, axis, [(i, i ^ mask) for i in range(lax.axis_size(axis))])


def digits(count):
    found = [(0, 2)]
    shift = 1
    while 1 << shift < count:
        radix = 4 if count >> shift >= 4 else 2
        found.append((shift, radix))
        shift += radix // 2
    return found


def turned(parts, digit):
    bit = 1
    while bit < len(parts):
        flag = digit & bit != 0
        parts = [jnp.where(flag, parts[r ^ bit], parts[r]) for r in range(len(parts))]
        bit *= 2
    return parts


def collected(block, awaited=None):
    cells = block[None]
    steps = [("seq", shift, radix) for shift, radix in reversed(digits(lax.axis_size("seq")))]
    steps += [("trk", 1, 2), ("trk", 0, 2)]
    for axis, shift, radix in steps:
        if awaited is not None and (axis, shift) == ("trk", 1):
            cells = after(cells, awaited)
        parts = [cells] + [partner(cells, axis, r << shift) for r in range(1, radix)]
        parts = turned(parts, lax.axis_index(axis) >> shift)
        cells = jnp.stack(parts, 1).reshape((-1,) + block.shape)
    return cells


def begun_digits(total, steps):
    radix = steps[0][1]
    parts = total.reshape((radix, -1) + total.shape[1:])
    return parts[0].astype(jnp.float32), [parts[r].astype(jnp.bfloat16) for r in range(1, radix)]


def ended_digits(begun, steps, awaited=()):
    total, sent = begun
    for place, (shift, radix) in enumerate(steps):
        if place:
            total, sent = begun_digits(total, steps[place:])
        for r in range(1, radix):
            got = partner(sent[r - 1], "seq", r << shift)
            for other in awaited:
                got = after(got, other)
            total = total + got.astype(jnp.float32)
    return total


def relative(cells, axis, digit):
    parts = [lax.index_in_dim(cells, r, axis, keepdims=False) for r in range(cells.shape[axis])]
    return jnp.stack(turned(parts, digit), axis)


def split(cells, at, axis, shift):
    digit = lax.axis_index(axis) >> shift & 1
    pick = lambda r: lax.dynamic_index_in_dim(cells, digit ^ r, at, keepdims=False)
    return pick(0).astype(jnp.float32), pick(1).astype(jnp.bfloat16)


def joined(kept, sent, axis, shift, awaited=None):
    got = partner(sent, axis, 1 << shift)
    if awaited is not None:
        got = after(got, awaited)
    return kept + got.astype(jnp.float32)


def relative_blocks(cells):
    steps = digits(lax.axis_size("seq"))[1:]
    shape = cells.shape[1:]
    cells = cells.reshape(tuple(radix for _, radix in reversed(steps)) + shape)
    for place, (shift, radix) in enumerate(steps):
        cells = relative(cells, len(steps) - 1 - place, lax.axis_index("seq") >> shift)
    cells = cells.transpose(tuple(range(len(steps) - 1, -1, -1)) + (len(steps), len(steps) + 1))
    return cells.reshape((-1,) + shape[1:])


def relative_rows(features):
    steps = digits(lax.axis_size("seq"))
    columns = features.shape[1]
    count = len(steps)
    cells = features.reshape(tuple(radix for _, radix in reversed(steps)) + (-1, columns))
    for place, (shift, radix) in enumerate(steps):
        cells = relative(cells, count - 1 - place, lax.axis_index("seq") >> shift)
    cells = cells.transpose(tuple(range(count - 1, -1, -1)) + (count, count + 1))
    return cells.reshape(-1, columns)


def after(cells, other):
    return cells + (other[(slice(0, 1),) * other.ndim].reshape((1,) * cells.ndim) * 0).astype(cells.dtype)


def window_exchanged(cells, awaited=None):
    sent = cells[2:]
    got = partner(sent if awaited is None else after(sent, awaited), "trk", 2)
    sibling = partner(jnp.stack([cells[1], got[1]]), "trk", 1)
    return [cells[0], sibling[0], got[0], sibling[1]]


def by_relation(cells):
    me = lax.axis_index("trk")
    return jnp.stack([lax.dynamic_index_in_dim(cells, me ^ r, 0, keepdims=False) for r in range(4)])


def weights_kernel(quarter, me, human, mouse, out, wide, small):
    wide[:, -128:] = jnp.zeros_like(wide[:, -128:])
    small[:, -256:] = jnp.zeros_like(small[:, -256:])
    wide[:, : human.shape[1]] = human[...]
    small[:, : mouse.shape[1]] = mouse[...]
    for at in range(4):
        cells = jnp.concatenate(
            [
                wide[:, 2 * at * quarter : 2 * (at + 1) * quarter],
                wide[:, (8 + at) * quarter : (9 + at) * quarter],
                small[:, at * quarter : (at + 1) * quarter],
            ],
            1,
        )
        out[me[0] ^ at] = cells.astype(jnp.bfloat16)


def window_weights(human, mouse, quarter):
    rows = human.shape[0]
    full = lambda cells: pl.BlockSpec(cells.shape, lambda i, me: (0, 0))
    shape = (4, rows, 4 * quarter)
    return pl.pallas_call(
        functools.partial(weights_kernel, quarter),
        grid_spec=pltpu.PrefetchScalarGridSpec(
            num_scalar_prefetch=1,
            grid=(1,),
            in_specs=[full(human), full(mouse)],
            out_specs=pl.BlockSpec(shape, lambda i, me: (0, 0, 0)),
            scratch_shapes=[
                pltpu.VMEM((rows, 12 * quarter), jnp.float32),
                pltpu.VMEM((rows, 4 * quarter), jnp.float32),
            ],
        ),
        out_shape=jax.ShapeDtypeStruct(shape, jnp.bfloat16),
        compiler_params=pltpu.CompilerParams(vmem_limit_bytes=24 * 2**20),
    )(lax.axis_index("trk").astype(jnp.int32).reshape(1), human, mouse)


def cots_kernel(human_cols, mouse_cols, scalars, first, last, mouse, out):
    at = pl.program_id(0)
    quarter = last.shape[0]
    row = at * quarter + lax.broadcasted_iota(jnp.int32, last.shape, 0)

    @pl.when(scalars[1] != 0)
    def _():
        out[0, : 2 * quarter] = first[...]
        cells = jnp.where(row < human_cols - 8 * quarter, last[...].astype(jnp.float32), 0.0)
        out[0, 2 * quarter :] = cells.astype(jnp.bfloat16)

    @pl.when(scalars[1] == 0)
    def _():
        out[0, : 2 * quarter] = jnp.zeros_like(first)
        cells = jnp.where(row < mouse_cols, mouse[...].astype(jnp.float32), 0.0)
        out[0, 2 * quarter :] = cells.astype(jnp.bfloat16)


def window_cots(human_flag, human, mouse, quarter):
    bins = human.shape[1]
    scalars = jnp.stack([lax.axis_index("trk"), human_flag]).astype(jnp.int32)
    return pl.pallas_call(
        functools.partial(cots_kernel, human.shape[0], mouse.shape[0]),
        grid_spec=pltpu.PrefetchScalarGridSpec(
            num_scalar_prefetch=1,
            grid=(4,),
            in_specs=[
                pl.BlockSpec((2 * quarter, bins), lambda i, scalars: (i, 0)),
                pl.BlockSpec((quarter, bins), lambda i, scalars: (8 + i, 0)),
                pl.BlockSpec((quarter, bins), lambda i, scalars: (i, 0)),
            ],
            out_specs=pl.BlockSpec((1, 3 * quarter, bins), lambda i, scalars: (scalars[0] ^ i, 0, 0)),
        ),
        out_shape=jax.ShapeDtypeStruct((4, 3 * quarter, bins), jnp.bfloat16),
        compiler_params=pltpu.CompilerParams(vmem_limit_bytes=24 * 2**20),
    )(scalars, human, human, mouse)


def window_bins(cells):
    got = partner(cells, "trk", 2)
    return jnp.concatenate([cells, got, partner(cells, "trk", 1), partner(got, "trk", 1)], 1)


def window_summed(cells):
    half = cells.shape[1] // 2
    quarter = half // 2
    kept = cells[:, :half].astype(jnp.float32)
    kept = kept + partner(cells[:, half:], "trk", 1).astype(jnp.float32)
    sent = kept[:, quarter:].astype(jnp.bfloat16)
    return kept[:, :quarter] + partner(sent, "trk", 2).astype(jnp.float32)


def window_returned(cells, awaited):
    half = cells.shape[1] // 2
    quarter = half // 2
    sibling = partner(cells[:, half:], "trk", 1)
    sent = jnp.stack([cells[:, quarter:half], sibling[:, quarter:]])
    return [cells[:, :quarter], sibling[:, :quarter]], partner(after(sent, awaited), "trk", 2)


def product(left, right):
    return lax.dot_general(left, right, (((1,), (1,)), ((), ())), preferred_element_type=jnp.float32)


def own_rows(total):
    parts = window_exchanged(by_relation(total.reshape(4, -1, total.shape[1])))
    return turned(parts, lax.axis_index("trk"))


def head_kernel(flag, features, weights, cots, out_first, out_last, total, gradient):
    columns = out_last.shape[0]
    wide = -(-columns // 128) * 128
    human = flag[0] != 0

    def run(first, count, cotangents):
        logits = lax.dot_general(
            weights[:, first : first + count],
            features[...],
            (((0,), (0,)), ((), ())),
            preferred_element_type=jnp.float32,
        )
        small = jnp.exp(-jnp.abs(logits))
        sigmoid = jnp.where(logits >= 0, 1.0, small) / (1.0 + small)
        predicted = (jnp.maximum(logits, 0.0) + jnp.log1p(small)).astype(jnp.bfloat16)
        return predicted, (cotangents.astype(jnp.float32) * sigmoid).astype(jnp.bfloat16)

    def back(first, slopes):
        last = first + slopes.shape[0]
        total[...] = jnp.dot(
            weights[:, first:last], slopes, preferred_element_type=jnp.float32
        ).astype(jnp.bfloat16)
        gradient[:, first:last] = product(features[...], slopes).astype(jnp.bfloat16)
        if first:
            gradient[:, :first] = jnp.zeros_like(gradient[:, :first])
        if last < gradient.shape[1]:
            gradient[:, last:] = jnp.zeros_like(gradient[:, last:])

    gap = jnp.zeros((wide - columns, cots.shape[1]), cots.dtype)

    @pl.when(human)
    def _():
        predicted, first = run(0, 2 * columns, cots[: 2 * columns, :])
        out_first[...] = predicted
        predicted, last = run(2 * columns, wide, jnp.concatenate([cots[2 * columns :, :], gap], 0))
        out_last[...] = predicted[:columns]
        back(0, jnp.concatenate([first, last], 0))

    @pl.when(jnp.logical_not(human))
    def _():
        start = 4 * columns - wide
        predicted, last = run(start, wide, jnp.concatenate([gap, cots[2 * columns :, :]], 0))
        out_first[...] = jnp.zeros_like(out_first)
        out_last[...] = predicted[wide - columns :]
        back(start, last)


def heads_part(flag, features, heads, cots):
    depth, bins = features.shape
    columns = cots.shape[0] // 3
    full = lambda shape: pl.BlockSpec(shape, lambda i, flag: (0, 0))
    shapes = [(2 * columns, bins), (columns, bins), (depth, bins), (depth, 4 * columns)]
    return pl.pallas_call(
        head_kernel,
        grid_spec=pltpu.PrefetchScalarGridSpec(
            num_scalar_prefetch=1,
            grid=(1,),
            in_specs=[full(features.shape), full(heads.shape), full(cots.shape)],
            out_specs=[full(shape) for shape in shapes],
        ),
        out_shape=[jax.ShapeDtypeStruct(shape, jnp.bfloat16) for shape in shapes],
        compiler_params=pltpu.CompilerParams(vmem_limit_bytes=60 * 2**20),
    )(flag, features, heads, cots)


def lanes(cells):
    sums = jnp.sum(cells, tuple(range(cells.ndim - 1)))
    return jnp.sum(jnp.pad(sums, (0, -sums.shape[0] % 128)).reshape(-1, 128), 0)


def moments(momentum_old, variance_old, gradient):
    momentum = beta_first * momentum_old + (1.0 - beta_first) * gradient
    variance = beta_second * variance_old + (1.0 - beta_second) * gradient * gradient
    direction = (
        momentum
        / (1.0 - beta_first**STEP)
        / (jnp.sqrt(variance / (1.0 - beta_second**STEP)) + adam_eps)
    )
    return (momentum, variance, direction)


def head_moments_kernel(quarter, *refs):
    cells, rest = refs[:4], refs[4:]
    early, states, spread, results, wide = rest[0], rest[1:7], rest[7], rest[8:14], rest[14]
    parts = [ref[...].astype(jnp.float32) for ref in cells]
    human = [part[:, : 2 * quarter] for part in parts] + [part[:, 2 * quarter : 3 * quarter] for part in parts]
    mouse = [part[:, 3 * quarter :] for part in parts]
    squares = []
    for at, pieces in enumerate((human, mouse)):
        weight, first, second = states[3 * at : 3 * at + 3]
        momentum_out, variance_out, update_out = results[3 * at : 3 * at + 3]
        columns = weight.shape[1]
        gradient = jnp.concatenate(pieces, 1)[:, :columns]
        momentum, variance, direction = moments(first[...], second[...], gradient)
        update = direction + decay_rate * weight[...]
        momentum_out[...] = momentum
        variance_out[...] = variance
        update_out[...] = update
        whole = columns // 128 * 128
        full = -(-columns // 128) * 128
        wide[:, whole:full] = jnp.zeros_like(wide[:, whole:full])
        wide[:, :columns] = update * update
        total = wide[:, :128]
        for start in range(128, full, 128):
            total = total + wide[:, start : start + 128]
        squares.append(jnp.sum(total, 0, keepdims=True))
    sums = jnp.concatenate([early[...]] + squares, 0)
    spread[...] = jnp.broadcast_to(sums[None], spread.shape)


def head_moments(quarter, devices, cells, early, states):
    full = lambda shape: pl.BlockSpec(shape, lambda i: (0,) * len(shape))
    operands = [*cells, early, *states]
    rows = states[0].shape[0]
    shapes = [(devices, early.shape[0] + 2, 128)] + [states[0].shape] * 3 + [states[3].shape] * 3
    return pl.pallas_call(
        functools.partial(head_moments_kernel, quarter),
        grid=(1,),
        in_specs=[full(operand.shape) for operand in operands],
        out_specs=[full(shape) for shape in shapes],
        out_shape=[jax.ShapeDtypeStruct(shape, jnp.float32) for shape in shapes],
        scratch_shapes=[pltpu.VMEM((rows, 12 * quarter), jnp.float32)],
        compiler_params=pltpu.CompilerParams(vmem_limit_bytes=48 * 2**20),
    )(*operands)


def updates_kernel(sums, *refs):
    count = 5
    weights, updates = refs[:count], refs[count : 2 * count]
    stats, results = refs[2 * count], refs[2 * count + 1 :]
    norms = jnp.sqrt(jnp.sum(sums[...], 1, keepdims=True))
    weight_norm, update_norm = norms[:count], norms[count:]
    ratio = weight_norm / (update_norm + adam_eps)
    lane = lax.broadcasted_iota(jnp.int32, stats.shape, 1)
    stats[...] = jnp.where(lane == 0, weight_norm, jnp.where(lane == 1, update_norm, ratio))
    for at in range(count):
        factor = matrix_rate * ratio[at : at + 1]
        if len(weights[at].shape) == 3:
            factor = factor[None]
        results[at][...] = weights[at][...] - factor * updates[at][...]


def updated_weights(sums, weights, updates):
    full = lambda shape: pl.BlockSpec(shape, lambda i: (0,) * len(shape))
    operands = [sums, *weights, *updates]
    shapes = [(5, 128)] + [weight.shape for weight in weights]
    return pl.pallas_call(
        updates_kernel,
        grid=(1,),
        in_specs=[full(operand.shape) for operand in operands],
        out_specs=[full(shape) for shape in shapes],
        out_shape=[jax.ShapeDtypeStruct(shape, jnp.float32) for shape in shapes],
        compiler_params=pltpu.CompilerParams(vmem_limit_bytes=32 * 2**20),
    )(*operands)


def body(
    bins,
    species,
    cot_human,
    cot_mouse,
    norm_params,
    norm_first,
    norm_second,
    dilated_weight,
    dilated_first,
    dilated_second,
    point_weight,
    point_first,
    point_second,
    final_weight,
    final_first,
    final_second,
    human_weight,
    human_first,
    human_second,
    mouse_weight,
    mouse_first,
    mouse_second,
):
    window_rows = bins.shape[0]
    seq_count = lax.axis_size("seq")
    trk_count = lax.axis_size("trk")
    total_rows = window_rows * seq_count * trk_count
    window_len = WINDOW_BINS
    first_row = lax.axis_index(("seq", "trk")) * window_rows
    window_id = first_row // window_len
    human_flag = lax.dynamic_index_in_dim(species, window_id, keepdims=False) == 0
    devices = seq_count * trk_count
    low = jnp.bfloat16
    human_cols = cot_human.shape[1]
    mouse_cols = cot_mouse.shape[1]
    quarter = -(-human_cols // 768) * 64
    chunk = 4 * quarter
    heads = window_exchanged(window_weights(human_weight, mouse_weight, quarter))
    heads_arrived = heads[2]
    heads_window = jnp.concatenate(turned(heads, lax.axis_index("trk")))
    heads = lax.all_gather(heads_window, "seq", axis=0, tiled=True)
    cots = window_cots(human_flag, cot_human.T, cot_mouse.T, quarter)
    own = dilated_weight.shape[1]
    low_params = norm_params.astype(low)
    low_params = jnp.pad(low_params, (0, 8 * B - low_params.shape[0])).reshape(8, B)
    early = jnp.concatenate([dilated_weight.astype(low).reshape(-1, B), low_params])
    final_low = final_weight.T.astype(low)
    late = jnp.concatenate([point_weight.T.astype(low), final_low[:, :B], final_low[:, B:]])
    early = collected(early)
    dilated_full = early[:, : 3 * own].reshape(devices, 3, own, B).transpose(1, 0, 2, 3)
    dilated_full = dilated_full.reshape(3, C, B)
    params = early[:, 3 * own, : norm_params.shape[0]].reshape(-1).astype(jnp.float32)
    gain_one = params[:C]
    shift_one = params[C : 2 * C]
    gain_two = params[2 * C : 2 * C + B]
    shift_two = params[2 * C + B :]
    values = bins.astype(jnp.float32)
    one_stats = everywhere(jnp.stack([jnp.sum(values, 0), jnp.sum(values * values, 0)]))
    mean_one = one_stats[0] / total_rows
    inverse_one = lax.rsqrt(one_stats[1] / total_rows - mean_one * mean_one + bn_eps)
    normed_one = (values - mean_one) * inverse_one
    affine_one = normed_one * gain_one + shift_one
    first_hidden = jax.nn.gelu(affine_one).astype(jnp.bfloat16)
    tap_positions = first_row - DILATION_GAP + jnp.arange(window_rows + 2 * DILATION_GAP)
    interior_slice = (jnp.floor_divide(tap_positions, window_len) == window_id).astype(
        jnp.bfloat16
    )[:, None]
    padded_input = extended(first_hidden, (("trk", 0),), DILATION_GAP) * interior_slice
    middle = jnp.zeros((window_rows, B), jnp.float32)
    for kernel_tap_index in range(3):
        middle = middle + jnp.dot(
            padded_input[
                kernel_tap_index * DILATION_GAP : kernel_tap_index * DILATION_GAP + window_rows
            ],
            dilated_full[kernel_tap_index],
            preferred_element_type=jnp.float32,
        )
    two_local = jnp.stack([jnp.sum(middle, 0), jnp.sum(middle * middle, 0)])
    two_stats = everywhere(two_local)
    late = collected(after(late, heads_arrived), two_stats)
    point_full = late[:, :own].reshape(C, B)
    final_full = jnp.concatenate(
        [late[:, own : 3 * own].reshape(-1, B), late[:, 3 * own :].reshape(-1, B)], 1
    )
    cots = window_exchanged(cots, two_stats)
    cots = jnp.concatenate([cots[0], cots[2], cots[1], cots[3]], 1)
    mean_two = two_stats[0] / total_rows
    inverse_two = lax.rsqrt(two_stats[1] / total_rows - mean_two * mean_two + bn_eps)
    normed_two = (middle - mean_two) * inverse_two
    affine_two = normed_two * gain_two + shift_two
    hidden_two = jax.nn.gelu(affine_two).astype(jnp.bfloat16)
    residual = values + contract_cols(hidden_two, point_full)
    residual_low = residual.astype(jnp.bfloat16)
    lifted = contract_cols(residual_low, final_full)
    features = jax.nn.gelu(lifted).astype(jnp.bfloat16)
    bins_features = window_bins(features.T)
    first_out, last_out, part, head_grads = heads_part(
        human_flag.astype(jnp.int32).reshape(1), bins_features, heads, cots
    )
    head_sum = lax.psum_scatter(head_grads, "seq", scatter_dimension=0, tiled=True)
    part = window_summed(part)
    predicted, predicted_arrived = window_returned(jnp.concatenate([first_out, last_out]), part)
    part = part.T
    lifted_grad = gelu_back(lifted, part).astype(jnp.bfloat16)
    final_grad = contracted_rows(lifted_grad, residual_low)
    residual_grad = jnp.dot(lifted_grad, final_full, preferred_element_type=jnp.float32)
    branch_grad = residual_grad.astype(jnp.bfloat16)
    point_grad = contracted_rows(branch_grad, hidden_two)
    affine_two_grad = gelu_back(
        affine_two, jnp.dot(branch_grad, point_full, preferred_element_type=jnp.float32)
    )
    two_back = everywhere(
        jnp.stack([jnp.sum(affine_two_grad * normed_two, 0), jnp.sum(affine_two_grad, 0)])
    )
    higher = digits(seq_count)[1:]
    two_back = after(two_back, predicted_arrived)
    central_gradient = (
        gain_two
        * inverse_two
        * (affine_two_grad - two_back[1] / total_rows - normed_two * two_back[0] / total_rows)
    ).astype(jnp.bfloat16)
    padded_gradient = extended(central_gradient, (("trk", 0),), DILATION_GAP) * interior_slice
    hidden_one_grad = jnp.zeros((window_rows, C), jnp.float32)
    tap_grads = []
    for kernel_tap_index in range(3):
        tap_shift = (2 - kernel_tap_index) * DILATION_GAP
        hidden_one_grad = hidden_one_grad + contract_cols(
            padded_gradient[tap_shift : tap_shift + window_rows], dilated_full[kernel_tap_index]
        )
        tap_grads.append(
            contracted_rows(
                padded_input[
                    kernel_tap_index * DILATION_GAP : kernel_tap_index * DILATION_GAP + window_rows
                ],
                central_gradient,
            )
        )
    dilated_grad = jnp.stack(tap_grads)
    affine_one_grad = gelu_back(affine_one, hidden_one_grad)
    one_local = jnp.concatenate(
        [jnp.sum(affine_one_grad * normed_one, 0), jnp.sum(affine_one_grad, 0)]
    )
    final_grad = final_grad.astype(low)
    trunk_grads = jnp.concatenate(
        [
            dilated_grad.astype(low).reshape(3, devices, own, B).transpose(1, 0, 2, 3).reshape(devices, -1, B),
            point_grad.astype(low).reshape(devices, own, B),
            final_grad[:, :B].reshape(devices, -1, B),
            final_grad[:, B:].reshape(devices, -1, B),
        ],
        1,
    )
    trunk_grads = trunk_grads.reshape((-1, 2, 2, 2) + trunk_grads.shape[1:])
    core = joined(*split(trunk_grads, 3, "trk", 0), "trk", 0)
    half = core.shape[3] // 2
    first, first_sent = split(core[:, :, :, :half], 2, "trk", 1)
    second, second_sent = split(core[:, :, :, half:], 1, "seq", 0)
    first = joined(first, first_sent, "trk", 1)
    second = joined(second, second_sent, "seq", 0)
    first, first_sent = split(first, 1, "seq", 0)
    second, second_sent = split(second, 1, "trk", 1)
    trunk_near = jnp.concatenate(
        [joined(first, first_sent, "seq", 0), joined(second, second_sent, "trk", 1)], 1
    )
    trunk_begun = begun_digits(relative_blocks(trunk_near), higher)
    trunk_sum = ended_digits(trunk_begun, higher)
    head_rows = own_rows(head_sum)
    dilated_sum = trunk_sum[: 3 * own].reshape(3, own, B)
    point_sum = trunk_sum[3 * own : 4 * own].T
    final_sum = jnp.concatenate([trunk_sum[4 * own : 6 * own], trunk_sum[6 * own :]], 1).T
    matrices = [
        (dilated_weight, dilated_first, dilated_second, dilated_sum),
        (point_weight, point_first, point_second, point_sum),
        (final_weight, final_first, final_second, final_sum),
    ]
    results = []
    weight_squares = []
    update_squares = []
    for kernel_weight, momentum_old, variance_old, gradient in matrices:
        momentum, variance, direction = moments(momentum_old, variance_old, gradient)
        update = direction + decay_rate * kernel_weight
        results.append((momentum, variance, update, kernel_weight))
        tall = kernel_weight.shape[0] > kernel_weight.shape[1] and kernel_weight.ndim == 2
        weight_squares.append(lanes((kernel_weight * kernel_weight).T if tall else kernel_weight * kernel_weight))
        update_squares.append(lanes((update * update).T if tall else update * update))
    head_states = (human_weight, human_first, human_second, mouse_weight, mouse_first, mouse_second)
    head_squares = [lanes(human_weight * human_weight), lanes(mouse_weight * mouse_weight)]
    early = jnp.stack(weight_squares + head_squares + update_squares)
    early = jnp.concatenate([one_local.reshape(-1, 128), early])
    spread, *head_results = head_moments(quarter, devices, head_rows, early, head_states)
    predicted_arrived = after(predicted_arrived, spread)
    predicted = turned(predicted + [predicted_arrived[0], predicted_arrived[1]], lax.axis_index("trk"))
    human_rows = human_flag.astype(jnp.float32)
    human_output = jnp.concatenate(
        [cells[: 2 * quarter] for cells in predicted] + [cells[2 * quarter :] for cells in predicted]
    )
    human_output = (human_output[:human_cols].astype(jnp.float32) * human_rows).T
    mouse_output = jnp.concatenate([cells[2 * quarter :] for cells in predicted])
    mouse_output = (mouse_output[:mouse_cols].astype(jnp.float32) * (1.0 - human_rows)).T
    last_sums = jnp.sum(lax.all_to_all(spread, ("seq", "trk"), 0, 0, tiled=True), 0)
    results.append(tuple(head_results[:3]) + (human_weight,))
    results.append(tuple(head_results[3:]) + (mouse_weight,))
    one_back = last_sums[: 2 * C // 128].reshape(2, C)
    input_grad = residual_grad + gain_one * inverse_one * (
        affine_one_grad - one_back[1] / total_rows - normed_one * one_back[0] / total_rows
    )
    norm_full = jnp.concatenate([one_back[0], one_back[1], two_back[0], two_back[1]])
    shard_len = norm_params.shape[0]
    norm_grad = lax.dynamic_slice_in_dim(
        norm_full, lax.axis_index(("seq", "trk")) * shard_len, shard_len
    )
    norm_momentum, norm_variance, norm_direction = moments(norm_first, norm_second, norm_grad)
    norm_updated = norm_params - norm_rate * norm_direction
    turns = (None, True, True, None, None)
    stats, *updated = updated_weights(
        last_sums[2 * C // 128 :],
        [entry[3].T if turn else entry[3] for entry, turn in zip(results, turns)],
        [entry[2].T if turn else entry[2] for entry, turn in zip(results, turns)],
    )
    updated = [cells.T if turn else cells for cells, turn in zip(updated, turns)]
    trust_stats = stats[:, :3].T
    return (
        human_output,
        mouse_output,
        input_grad,
        norm_momentum,
        norm_variance,
        norm_updated,
        results[0][0],
        results[0][1],
        updated[0],
        results[1][0],
        results[1][1],
        updated[1],
        results[2][0],
        results[2][1],
        updated[2],
        results[3][0],
        results[3][1],
        updated[3],
        results[4][0],
        results[4][1],
        updated[4],
        trust_stats,
    )


def solution(mesh):
    in_specs = (
        P(("seq", "trk"), None),
        P(),
        P(("seq", "trk"), None),
        P(("seq", "trk"), None),
        P(("seq", "trk")),
        P(("seq", "trk")),
        P(("seq", "trk")),
        P(None, ("seq", "trk"), None),
        P(None, ("seq", "trk"), None),
        P(None, ("seq", "trk"), None),
        P(None, ("seq", "trk")),
        P(None, ("seq", "trk")),
        P(None, ("seq", "trk")),
        P(None, ("seq", "trk")),
        P(None, ("seq", "trk")),
        P(None, ("seq", "trk")),
        P(("seq", "trk"), None),
        P(("seq", "trk"), None),
        P(("seq", "trk"), None),
        P(("seq", "trk"), None),
        P(("seq", "trk"), None),
        P(("seq", "trk"), None),
    )
    out_specs = (
        P(("seq", "trk"), None),
        P(("seq", "trk"), None),
        P(("seq", "trk"), None),
        P(("seq", "trk")),
        P(("seq", "trk")),
        P(("seq", "trk")),
        P(None, ("seq", "trk"), None),
        P(None, ("seq", "trk"), None),
        P(None, ("seq", "trk"), None),
        P(None, ("seq", "trk")),
        P(None, ("seq", "trk")),
        P(None, ("seq", "trk")),
        P(None, ("seq", "trk")),
        P(None, ("seq", "trk")),
        P(None, ("seq", "trk")),
        P(("seq", "trk"), None),
        P(("seq", "trk"), None),
        P(("seq", "trk"), None),
        P(("seq", "trk"), None),
        P(("seq", "trk"), None),
        P(("seq", "trk"), None),
        P(),
    )
    return jax.shard_map(body, mesh=mesh, in_specs=in_specs, out_specs=out_specs, check_vma=False)
```

```python
import functools

import jax
import jax.numpy as jnp
from jax import lax
from jax.experimental import pallas as pl
from jax.experimental.pallas import tpu as pltpu
from jax.sharding import PartitionSpec as P

C = 768
B = 384
DILATION_GAP = 57
WINDOW_BINS = 1024
STEP = 10


bn_eps = 1e-05
beta_first = 0.9
beta_second = 0.999
adam_eps = 1e-06
decay_rate = 0.01
matrix_rate = 0.5
norm_rate = 0.2


def extended(cells, sides, width):
    for axis, dim in sides:
        count = lax.axis_size(axis)
        ends = count - 1
        head = lax.slice_in_dim(cells, 0, width, axis=dim)
        tail = lax.slice_in_dim(cells, cells.shape[dim] - width, cells.shape[dim], axis=dim)
        cells = jnp.concatenate(
            [
                lax.ppermute(tail, axis, [(i, (i + 1) % count) for i in range(ends)]),
                cells,
                lax.ppermute(head, axis, [((i + 1) % count, i) for i in range(ends)]),
            ],
            axis=dim,
        )
    return cells


def gelu_back(inputs, gradient):
    unused, pullback = jax.vjp(jax.nn.gelu, inputs)
    return pullback(gradient)[0]


def contracted_rows(left, right):
    return lax.dot_general(
        left, right, (((0,), (0,)), ((), ())), preferred_element_type=jnp.float32
    )


def contract_cols(left, right):
    return lax.dot_general(
        left, right, (((1,), (1,)), ((), ())), preferred_element_type=jnp.float32
    )


def everywhere(vector):
    axes = ("seq", "trk")
    count = lax.axis_size("seq") * lax.axis_size("trk")
    spread = jnp.broadcast_to(vector[None], (count,) + vector.shape)
    return jnp.sum(lax.all_to_all(spread, axes, 0, 0, tiled=True), 0)


def partner(cells, axis, mask):
    return lax.ppermute(cells, axis, [(i, i ^ mask) for i in range(lax.axis_size(axis))])


def digits(count):
    found = [(0, 2)]
    shift = 1
    while 1 << shift < count:
        radix = 4 if count >> shift >= 4 else 2
        found.append((shift, radix))
        shift += radix // 2
    return found


def turned(parts, digit):
    bit = 1
    while bit < len(parts):
        flag = digit & bit != 0
        parts = [jnp.where(flag, parts[r ^ bit], parts[r]) for r in range(len(parts))]
        bit *= 2
    return parts


def collected(block, awaited=None):
    cells = block[None]
    steps = [("seq", shift, radix) for shift, radix in reversed(digits(lax.axis_size("seq")))]
    steps += [("trk", 1, 2), ("trk", 0, 2)]
    for axis, shift, radix in steps:
        if awaited is not None and (axis, shift) == ("trk", 1):
            cells = after(cells, awaited)
        parts = [cells] + [partner(cells, axis, r << shift) for r in range(1, radix)]
        parts = turned(parts, lax.axis_index(axis) >> shift)
        cells = jnp.stack(parts, 1).reshape((-1,) + block.shape)
    return cells


def begun_digits(total, steps):
    radix = steps[0][1]
    parts = total.reshape((radix, -1) + total.shape[1:])
    return parts[0].astype(jnp.float32), [parts[r].astype(jnp.bfloat16) for r in range(1, radix)]


def ended_digits(begun, steps, awaited=()):
    total, sent = begun
    for place, (shift, radix) in enumerate(steps):
        if place:
            total, sent = begun_digits(total, steps[place:])
        for r in range(1, radix):
            got = partner(sent[r - 1], "seq", r << shift)
            for other in awaited:
                got = after(got, other)
            total = total + got.astype(jnp.float32)
    return total


def relative(cells, axis, digit):
    parts = [lax.index_in_dim(cells, r, axis, keepdims=False) for r in range(cells.shape[axis])]
    return jnp.stack(turned(parts, digit), axis)


def split(cells, at, axis, shift):
    digit = lax.axis_index(axis) >> shift & 1
    pick = lambda r: lax.dynamic_index_in_dim(cells, digit ^ r, at, keepdims=False)
    return pick(0).astype(jnp.float32), pick(1).astype(jnp.bfloat16)


def joined(kept, sent, axis, shift, awaited=None):
    got = partner(sent, axis, 1 << shift)
    if awaited is not None:
        got = after(got, awaited)
    return kept + got.astype(jnp.float32)


def relative_blocks(cells):
    steps = digits(lax.axis_size("seq"))[1:]
    shape = cells.shape[1:]
    cells = cells.reshape(tuple(radix for _, radix in reversed(steps)) + shape)
    for place, (shift, radix) in enumerate(steps):
        cells = relative(cells, len(steps) - 1 - place, lax.axis_index("seq") >> shift)
    cells = cells.transpose(tuple(range(len(steps) - 1, -1, -1)) + (len(steps), len(steps) + 1))
    return cells.reshape((-1,) + shape[1:])


def relative_rows(features):
    steps = digits(lax.axis_size("seq"))
    columns = features.shape[1]
    count = len(steps)
    cells = features.reshape(tuple(radix for _, radix in reversed(steps)) + (-1, columns))
    for place, (shift, radix) in enumerate(steps):
        cells = relative(cells, count - 1 - place, lax.axis_index("seq") >> shift)
    cells = cells.transpose(tuple(range(count - 1, -1, -1)) + (count, count + 1))
    return cells.reshape(-1, columns)


def after(cells, other):
    return cells + (other[(slice(0, 1),) * other.ndim].reshape((1,) * cells.ndim) * 0).astype(cells.dtype)


def window_exchanged(cells, awaited=None):
    sent = cells[2:]
    got = partner(sent if awaited is None else after(sent, awaited), "trk", 2)
    sibling = partner(jnp.stack([cells[1], got[1]]), "trk", 1)
    return [cells[0], sibling[0], got[0], sibling[1]]


def by_relation(cells):
    me = lax.axis_index("trk")
    return jnp.stack([lax.dynamic_index_in_dim(cells, me ^ r, 0, keepdims=False) for r in range(4)])


def weights_kernel(quarter, me, human, mouse, out, wide, small):
    wide[:, -128:] = jnp.zeros_like(wide[:, -128:])
    small[:, -256:] = jnp.zeros_like(small[:, -256:])
    wide[:, : human.shape[1]] = human[...]
    small[:, : mouse.shape[1]] = mouse[...]
    for at in range(4):
        cells = jnp.concatenate(
            [
                wide[:, 2 * at * quarter : 2 * (at + 1) * quarter],
                wide[:, (8 + at) * quarter : (9 + at) * quarter],
                small[:, at * quarter : (at + 1) * quarter],
            ],
            1,
        )
        out[me[0] ^ at] = cells.astype(jnp.bfloat16)


def window_weights(human, mouse, quarter):
    rows = human.shape[0]
    full = lambda cells: pl.BlockSpec(cells.shape, lambda i, me: (0, 0))
    shape = (4, rows, 4 * quarter)
    return pl.pallas_call(
        functools.partial(weights_kernel, quarter),
        grid_spec=pltpu.PrefetchScalarGridSpec(
            num_scalar_prefetch=1,
            grid=(1,),
            in_specs=[full(human), full(mouse)],
            out_specs=pl.BlockSpec(shape, lambda i, me: (0, 0, 0)),
            scratch_shapes=[
                pltpu.VMEM((rows, 12 * quarter), jnp.float32),
                pltpu.VMEM((rows, 4 * quarter), jnp.float32),
            ],
        ),
        out_shape=jax.ShapeDtypeStruct(shape, jnp.bfloat16),
        compiler_params=pltpu.CompilerParams(vmem_limit_bytes=24 * 2**20),
    )(lax.axis_index("trk").astype(jnp.int32).reshape(1), human, mouse)


def cots_kernel(human_cols, mouse_cols, scalars, first, last, mouse, out):
    at = pl.program_id(0)
    quarter = last.shape[0]
    row = at * quarter + lax.broadcasted_iota(jnp.int32, last.shape, 0)

    @pl.when(scalars[1] != 0)
    def _():
        out[0, : 2 * quarter] = first[...]
        cells = jnp.where(row < human_cols - 8 * quarter, last[...].astype(jnp.float32), 0.0)
        out[0, 2 * quarter :] = cells.astype(jnp.bfloat16)

    @pl.when(scalars[1] == 0)
    def _():
        out[0, : 2 * quarter] = jnp.zeros_like(first)
        cells = jnp.where(row < mouse_cols, mouse[...].astype(jnp.float32), 0.0)
        out[0, 2 * quarter :] = cells.astype(jnp.bfloat16)


def window_cots(human_flag, human, mouse, quarter):
    bins = human.shape[1]
    scalars = jnp.stack([lax.axis_index("trk"), human_flag]).astype(jnp.int32)
    return pl.pallas_call(
        functools.partial(cots_kernel, human.shape[0], mouse.shape[0]),
        grid_spec=pltpu.PrefetchScalarGridSpec(
            num_scalar_prefetch=1,
            grid=(4,),
            in_specs=[
                pl.BlockSpec((2 * quarter, bins), lambda i, scalars: (i, 0)),
                pl.BlockSpec((quarter, bins), lambda i, scalars: (8 + i, 0)),
                pl.BlockSpec((quarter, bins), lambda i, scalars: (i, 0)),
            ],
            out_specs=pl.BlockSpec((1, 3 * quarter, bins), lambda i, scalars: (scalars[0] ^ i, 0, 0)),
        ),
        out_shape=jax.ShapeDtypeStruct((4, 3 * quarter, bins), jnp.bfloat16),
        compiler_params=pltpu.CompilerParams(vmem_limit_bytes=24 * 2**20),
    )(scalars, human, human, mouse)


def window_bins(cells):
    got = partner(cells, "trk", 2)
    return jnp.concatenate([cells, got, partner(cells, "trk", 1), partner(got, "trk", 1)], 1)


def window_summed(cells):
    half = cells.shape[1] // 2
    quarter = half // 2
    kept = cells[:, :half].astype(jnp.float32)
    kept = kept + partner(cells[:, half:], "trk", 1).astype(jnp.float32)
    sent = kept[:, quarter:].astype(jnp.bfloat16)
    return kept[:, :quarter] + partner(sent, "trk", 2).astype(jnp.float32)


def window_returned(cells, awaited):
    half = cells.shape[1] // 2
    quarter = half // 2
    sibling = partner(cells[:, half:], "trk", 1)
    sent = jnp.stack([cells[:, quarter:half], sibling[:, quarter:]])
    return [cells[:, :quarter], sibling[:, :quarter]], partner(after(sent, awaited), "trk", 2)


def product(left, right):
    return lax.dot_general(left, right, (((1,), (1,)), ((), ())), preferred_element_type=jnp.float32)


def own_rows(total):
    parts = window_exchanged(by_relation(total.reshape(4, -1, total.shape[1])))
    return turned(parts, lax.axis_index("trk"))


def head_kernel(flag, features, weights, cots, out_first, out_last, total, gradient):
    columns = out_last.shape[0]
    wide = -(-columns // 128) * 128
    human = flag[0] != 0

    def run(first, count, cotangents):
        logits = lax.dot_general(
            weights[:, first : first + count],
            features[...],
            (((0,), (0,)), ((), ())),
            preferred_element_type=jnp.float32,
        )
        small = jnp.exp(-jnp.abs(logits))
        sigmoid = jnp.where(logits >= 0, 1.0, small) / (1.0 + small)
        predicted = (jnp.maximum(logits, 0.0) + jnp.log1p(small)).astype(jnp.bfloat16)
        return predicted, (cotangents.astype(jnp.float32) * sigmoid).astype(jnp.bfloat16)

    def back(first, slopes):
        last = first + slopes.shape[0]
        total[...] = jnp.dot(
            weights[:, first:last], slopes, preferred_element_type=jnp.float32
        ).astype(jnp.bfloat16)
        gradient[:, first:last] = product(features[...], slopes).astype(jnp.bfloat16)
        if first:
            gradient[:, :first] = jnp.zeros_like(gradient[:, :first])
        if last < gradient.shape[1]:
            gradient[:, last:] = jnp.zeros_like(gradient[:, last:])

    gap = jnp.zeros((wide - columns, cots.shape[1]), cots.dtype)

    @pl.when(human)
    def _():
        predicted, first = run(0, 2 * columns, cots[: 2 * columns, :])
        out_first[...] = predicted
        predicted, last = run(2 * columns, wide, jnp.concatenate([cots[2 * columns :, :], gap], 0))
        out_last[...] = predicted[:columns]
        back(0, jnp.concatenate([first, last], 0))

    @pl.when(jnp.logical_not(human))
    def _():
        start = 4 * columns - wide
        predicted, last = run(start, wide, jnp.concatenate([gap, cots[2 * columns :, :]], 0))
        out_first[...] = jnp.zeros_like(out_first)
        out_last[...] = predicted[wide - columns :]
        back(start, last)


def heads_part(flag, features, heads, cots):
    depth, bins = features.shape
    columns = cots.shape[0] // 3
    full = lambda shape: pl.BlockSpec(shape, lambda i, flag: (0, 0))
    shapes = [(2 * columns, bins), (columns, bins), (depth, bins), (depth, 4 * columns)]
    return pl.pallas_call(
        head_kernel,
        grid_spec=pltpu.PrefetchScalarGridSpec(
            num_scalar_prefetch=1,
            grid=(1,),
            in_specs=[full(features.shape), full(heads.shape), full(cots.shape)],
            out_specs=[full(shape) for shape in shapes],
        ),
        out_shape=[jax.ShapeDtypeStruct(shape, jnp.bfloat16) for shape in shapes],
        compiler_params=pltpu.CompilerParams(vmem_limit_bytes=60 * 2**20),
    )(flag, features, heads, cots)


def lanes(cells):
    sums = jnp.sum(cells, tuple(range(cells.ndim - 1)))
    return jnp.sum(jnp.pad(sums, (0, -sums.shape[0] % 128)).reshape(-1, 128), 0)


def moments(momentum_old, variance_old, gradient):
    momentum = beta_first * momentum_old + (1.0 - beta_first) * gradient
    variance = beta_second * variance_old + (1.0 - beta_second) * gradient * gradient
    direction = (
        momentum
        / (1.0 - beta_first**STEP)
        / (jnp.sqrt(variance / (1.0 - beta_second**STEP)) + adam_eps)
    )
    return (momentum, variance, direction)


def head_moments_kernel(quarter, *refs):
    cells, rest = refs[:4], refs[4:]
    early, states, spread, results, wide = rest[0], rest[1:7], rest[7], rest[8:14], rest[14]
    parts = [ref[...].astype(jnp.float32) for ref in cells]
    human = [part[:, : 2 * quarter] for part in parts] + [part[:, 2 * quarter : 3 * quarter] for part in parts]
    mouse = [part[:, 3 * quarter :] for part in parts]
    squares = []
    for at, pieces in enumerate((human, mouse)):
        weight, first, second = states[3 * at : 3 * at + 3]
        momentum_out, variance_out, update_out = results[3 * at : 3 * at + 3]
        columns = weight.shape[1]
        gradient = jnp.concatenate(pieces, 1)[:, :columns]
        momentum, variance, direction = moments(first[...], second[...], gradient)
        update = direction + decay_rate * weight[...]
        momentum_out[...] = momentum
        variance_out[...] = variance
        update_out[...] = update
        whole = columns // 128 * 128
        full = -(-columns // 128) * 128
        wide[:, whole:full] = jnp.zeros_like(wide[:, whole:full])
        wide[:, :columns] = update * update
        total = wide[:, :128]
        for start in range(128, full, 128):
            total = total + wide[:, start : start + 128]
        squares.append(jnp.sum(total, 0, keepdims=True))
    sums = jnp.concatenate([early[...]] + squares, 0)
    spread[...] = jnp.broadcast_to(sums[None], spread.shape)


def head_moments(quarter, devices, cells, early, states):
    full = lambda shape: pl.BlockSpec(shape, lambda i: (0,) * len(shape))
    operands = [*cells, early, *states]
    rows = states[0].shape[0]
    shapes = [(devices, early.shape[0] + 2, 128)] + [states[0].shape] * 3 + [states[3].shape] * 3
    return pl.pallas_call(
        functools.partial(head_moments_kernel, quarter),
        grid=(1,),
        in_specs=[full(operand.shape) for operand in operands],
        out_specs=[full(shape) for shape in shapes],
        out_shape=[jax.ShapeDtypeStruct(shape, jnp.float32) for shape in shapes],
        scratch_shapes=[pltpu.VMEM((rows, 12 * quarter), jnp.float32)],
        compiler_params=pltpu.CompilerParams(vmem_limit_bytes=48 * 2**20),
    )(*operands)


def updates_kernel(sums, *refs):
    count = 5
    weights, updates = refs[:count], refs[count : 2 * count]
    stats, results = refs[2 * count], refs[2 * count + 1 :]
    total = jnp.sum(sums[:, sums.shape[1] - 2 * count :, :], 0)
    norms = jnp.sqrt(jnp.sum(total, 1, keepdims=True))
    weight_norm, update_norm = norms[:count], norms[count:]
    ratio = weight_norm / (update_norm + adam_eps)
    lane = lax.broadcasted_iota(jnp.int32, stats.shape, 1)
    stats[...] = jnp.where(lane == 0, weight_norm, jnp.where(lane == 1, update_norm, ratio))
    for at in range(count):
        factor = matrix_rate * ratio[at : at + 1]
        if len(weights[at].shape) == 3:
            factor = factor[None]
        results[at][...] = weights[at][...] - factor * updates[at][...]


def updated_weights(sums, weights, updates):
    full = lambda shape: pl.BlockSpec(shape, lambda i: (0,) * len(shape))
    operands = [sums, *weights, *updates]
    shapes = [(5, 128)] + [weight.shape for weight in weights]
    return pl.pallas_call(
        updates_kernel,
        grid=(1,),
        in_specs=[full(operand.shape) for operand in operands],
        out_specs=[full(shape) for shape in shapes],
        out_shape=[jax.ShapeDtypeStruct(shape, jnp.float32) for shape in shapes],
        compiler_params=pltpu.CompilerParams(vmem_limit_bytes=32 * 2**20),
    )(*operands)


def body(
    bins,
    species,
    cot_human,
    cot_mouse,
    norm_params,
    norm_first,
    norm_second,
    dilated_weight,
    dilated_first,
    dilated_second,
    point_weight,
    point_first,
    point_second,
    final_weight,
    final_first,
    final_second,
    human_weight,
    human_first,
    human_second,
    mouse_weight,
    mouse_first,
    mouse_second,
):
    window_rows = bins.shape[0]
    seq_count = lax.axis_size("seq")
    trk_count = lax.axis_size("trk")
    total_rows = window_rows * seq_count * trk_count
    window_len = WINDOW_BINS
    first_row = lax.axis_index(("seq", "trk")) * window_rows
    window_id = first_row // window_len
    human_flag = lax.dynamic_index_in_dim(species, window_id, keepdims=False) == 0
    devices = seq_count * trk_count
    low = jnp.bfloat16
    human_cols = cot_human.shape[1]
    mouse_cols = cot_mouse.shape[1]
    quarter = -(-human_cols // 768) * 64
    chunk = 4 * quarter
    heads = window_exchanged(window_weights(human_weight, mouse_weight, quarter))
    heads_arrived = heads[2]
    heads_window = jnp.concatenate(turned(heads, lax.axis_index("trk")))
    heads = lax.all_gather(heads_window, "seq", axis=0, tiled=True)
    cots = window_cots(human_flag, cot_human.T, cot_mouse.T, quarter)
    own = dilated_weight.shape[1]
    low_params = norm_params.astype(low)
    low_params = jnp.pad(low_params, (0, 8 * B - low_params.shape[0])).reshape(8, B)
    early = jnp.concatenate([dilated_weight.astype(low).reshape(-1, B), low_params])
    final_low = final_weight.T.astype(low)
    late = jnp.concatenate([point_weight.T.astype(low), final_low[:, :B], final_low[:, B:]])
    early = collected(early)
    dilated_full = early[:, : 3 * own].reshape(devices, 3, own, B).transpose(1, 0, 2, 3)
    dilated_full = dilated_full.reshape(3, C, B)
    params = early[:, 3 * own, : norm_params.shape[0]].reshape(-1).astype(jnp.float32)
    gain_one = params[:C]
    shift_one = params[C : 2 * C]
    gain_two = params[2 * C : 2 * C + B]
    shift_two = params[2 * C + B :]
    values = bins.astype(jnp.float32)
    one_stats = everywhere(jnp.stack([jnp.sum(values, 0), jnp.sum(values * values, 0)]))
    mean_one = one_stats[0] / total_rows
    inverse_one = lax.rsqrt(one_stats[1] / total_rows - mean_one * mean_one + bn_eps)
    normed_one = (values - mean_one) * inverse_one
    affine_one = normed_one * gain_one + shift_one
    first_hidden = jax.nn.gelu(affine_one).astype(jnp.bfloat16)
    tap_positions = first_row - DILATION_GAP + jnp.arange(window_rows + 2 * DILATION_GAP)
    interior_slice = (jnp.floor_divide(tap_positions, window_len) == window_id).astype(
        jnp.bfloat16
    )[:, None]
    padded_input = extended(first_hidden, (("trk", 0),), DILATION_GAP) * interior_slice
    middle = jnp.zeros((window_rows, B), jnp.float32)
    for kernel_tap_index in range(3):
        middle = middle + jnp.dot(
            padded_input[
                kernel_tap_index * DILATION_GAP : kernel_tap_index * DILATION_GAP + window_rows
            ],
            dilated_full[kernel_tap_index],
            preferred_element_type=jnp.float32,
        )
    two_local = jnp.stack([jnp.sum(middle, 0), jnp.sum(middle * middle, 0)])
    two_stats = everywhere(two_local)
    late = collected(after(late, heads_arrived), two_stats)
    point_full = late[:, :own].reshape(C, B)
    final_full = jnp.concatenate(
        [late[:, own : 3 * own].reshape(-1, B), late[:, 3 * own :].reshape(-1, B)], 1
    )
    cots = window_exchanged(cots, two_stats)
    cots = jnp.concatenate([cots[0], cots[2], cots[1], cots[3]], 1)
    mean_two = two_stats[0] / total_rows
    inverse_two = lax.rsqrt(two_stats[1] / total_rows - mean_two * mean_two + bn_eps)
    normed_two = (middle - mean_two) * inverse_two
    affine_two = normed_two * gain_two + shift_two
    hidden_two = jax.nn.gelu(affine_two).astype(jnp.bfloat16)
    residual = values + contract_cols(hidden_two, point_full)
    residual_low = residual.astype(jnp.bfloat16)
    lifted = contract_cols(residual_low, final_full)
    features = jax.nn.gelu(lifted).astype(jnp.bfloat16)
    bins_features = window_bins(features.T)
    first_out, last_out, part, head_grads = heads_part(
        human_flag.astype(jnp.int32).reshape(1), bins_features, heads, cots
    )
    head_sum = lax.psum_scatter(head_grads, "seq", scatter_dimension=0, tiled=True)
    part = window_summed(part)
    predicted, predicted_arrived = window_returned(jnp.concatenate([first_out, last_out]), part)
    part = part.T
    lifted_grad = gelu_back(lifted, part).astype(jnp.bfloat16)
    final_grad = contracted_rows(lifted_grad, residual_low)
    residual_grad = jnp.dot(lifted_grad, final_full, preferred_element_type=jnp.float32)
    branch_grad = residual_grad.astype(jnp.bfloat16)
    point_grad = contracted_rows(branch_grad, hidden_two)
    affine_two_grad = gelu_back(
        affine_two, jnp.dot(branch_grad, point_full, preferred_element_type=jnp.float32)
    )
    two_back = everywhere(
        jnp.stack([jnp.sum(affine_two_grad * normed_two, 0), jnp.sum(affine_two_grad, 0)])
    )
    higher = digits(seq_count)[1:]
    two_back = after(two_back, predicted_arrived)
    central_gradient = (
        gain_two
        * inverse_two
        * (affine_two_grad - two_back[1] / total_rows - normed_two * two_back[0] / total_rows)
    ).astype(jnp.bfloat16)
    padded_gradient = extended(central_gradient, (("trk", 0),), DILATION_GAP) * interior_slice
    hidden_one_grad = jnp.zeros((window_rows, C), jnp.float32)
    tap_grads = []
    for kernel_tap_index in range(3):
        tap_shift = (2 - kernel_tap_index) * DILATION_GAP
        hidden_one_grad = hidden_one_grad + contract_cols(
            padded_gradient[tap_shift : tap_shift + window_rows], dilated_full[kernel_tap_index]
        )
        tap_grads.append(
            contracted_rows(
                padded_input[
                    kernel_tap_index * DILATION_GAP : kernel_tap_index * DILATION_GAP + window_rows
                ],
                central_gradient,
            )
        )
    dilated_grad = jnp.stack(tap_grads)
    affine_one_grad = gelu_back(affine_one, hidden_one_grad)
    one_local = jnp.concatenate(
        [jnp.sum(affine_one_grad * normed_one, 0), jnp.sum(affine_one_grad, 0)]
    )
    final_grad = final_grad.astype(low)
    trunk_grads = jnp.concatenate(
        [
            dilated_grad.astype(low).reshape(3, devices, own, B).transpose(1, 0, 2, 3).reshape(devices, -1, B),
            point_grad.astype(low).reshape(devices, own, B),
            final_grad[:, :B].reshape(devices, -1, B),
            final_grad[:, B:].reshape(devices, -1, B),
        ],
        1,
    )
    trunk_grads = trunk_grads.reshape((-1, 2, 2, 2) + trunk_grads.shape[1:])
    core = joined(*split(trunk_grads, 3, "trk", 0), "trk", 0)
    half = core.shape[3] // 2
    first, first_sent = split(core[:, :, :, :half], 2, "trk", 1)
    second, second_sent = split(core[:, :, :, half:], 1, "seq", 0)
    first = joined(first, first_sent, "trk", 1)
    second = joined(second, second_sent, "seq", 0)
    first, first_sent = split(first, 1, "seq", 0)
    second, second_sent = split(second, 1, "trk", 1)
    trunk_near = jnp.concatenate(
        [joined(first, first_sent, "seq", 0), joined(second, second_sent, "trk", 1)], 1
    )
    trunk_begun = begun_digits(relative_blocks(trunk_near), higher)
    trunk_sum = ended_digits(trunk_begun, higher)
    head_rows = own_rows(head_sum)
    dilated_sum = trunk_sum[: 3 * own].reshape(3, own, B)
    point_sum = trunk_sum[3 * own : 4 * own].T
    final_sum = jnp.concatenate([trunk_sum[4 * own : 6 * own], trunk_sum[6 * own :]], 1).T
    matrices = [
        (dilated_weight, dilated_first, dilated_second, dilated_sum),
        (point_weight, point_first, point_second, point_sum),
        (final_weight, final_first, final_second, final_sum),
    ]
    results = []
    weight_squares = []
    update_squares = []
    for kernel_weight, momentum_old, variance_old, gradient in matrices:
        momentum, variance, direction = moments(momentum_old, variance_old, gradient)
        update = direction + decay_rate * kernel_weight
        results.append((momentum, variance, update, kernel_weight))
        tall = kernel_weight.shape[0] > kernel_weight.shape[1] and kernel_weight.ndim == 2
        weight_squares.append(lanes((kernel_weight * kernel_weight).T if tall else kernel_weight * kernel_weight))
        update_squares.append(lanes((update * update).T if tall else update * update))
    head_states = (human_weight, human_first, human_second, mouse_weight, mouse_first, mouse_second)
    head_squares = [lanes(human_weight * human_weight), lanes(mouse_weight * mouse_weight)]
    early = jnp.stack(weight_squares + head_squares + update_squares)
    early = jnp.concatenate([one_local.reshape(-1, 128), early])
    spread, *head_results = head_moments(quarter, devices, head_rows, early, head_states)
    predicted_arrived = after(predicted_arrived, spread)
    predicted = turned(predicted + [predicted_arrived[0], predicted_arrived[1]], lax.axis_index("trk"))
    human_rows = human_flag.astype(jnp.float32)
    human_output = jnp.concatenate(
        [cells[: 2 * quarter] for cells in predicted] + [cells[2 * quarter :] for cells in predicted]
    )
    human_output = (human_output[:human_cols].astype(jnp.float32) * human_rows).T
    mouse_output = jnp.concatenate([cells[2 * quarter :] for cells in predicted])
    mouse_output = (mouse_output[:mouse_cols].astype(jnp.float32) * (1.0 - human_rows)).T
    arrived = lax.all_to_all(spread, ("seq", "trk"), 0, 0, tiled=True)
    last_sums = jnp.sum(arrived, 0)
    results.append(tuple(head_results[:3]) + (human_weight,))
    results.append(tuple(head_results[3:]) + (mouse_weight,))
    one_back = last_sums[: 2 * C // 128].reshape(2, C)
    input_grad = residual_grad + gain_one * inverse_one * (
        affine_one_grad - one_back[1] / total_rows - normed_one * one_back[0] / total_rows
    )
    norm_full = jnp.concatenate([one_back[0], one_back[1], two_back[0], two_back[1]])
    shard_len = norm_params.shape[0]
    norm_grad = lax.dynamic_slice_in_dim(
        norm_full, lax.axis_index(("seq", "trk")) * shard_len, shard_len
    )
    norm_momentum, norm_variance, norm_direction = moments(norm_first, norm_second, norm_grad)
    norm_updated = norm_params - norm_rate * norm_direction
    turns = (None, True, True, None, None)
    stats, *updated = updated_weights(
        arrived,
        [entry[3].T if turn else entry[3] for entry, turn in zip(results, turns)],
        [entry[2].T if turn else entry[2] for entry, turn in zip(results, turns)],
    )
    updated = [cells.T if turn else cells for cells, turn in zip(updated, turns)]
    trust_stats = stats[:, :3].T
    return (
        human_output,
        mouse_output,
        input_grad,
        norm_momentum,
        norm_variance,
        norm_updated,
        results[0][0],
        results[0][1],
        updated[0],
        results[1][0],
        results[1][1],
        updated[1],
        results[2][0],
        results[2][1],
        updated[2],
        results[3][0],
        results[3][1],
        updated[3],
        results[4][0],
        results[4][1],
        updated[4],
        trust_stats,
    )


def solution(mesh):
    in_specs = (
        P(("seq", "trk"), None),
        P(),
        P(("seq", "trk"), None),
        P(("seq", "trk"), None),
        P(("seq", "trk")),
        P(("seq", "trk")),
        P(("seq", "trk")),
        P(None, ("seq", "trk"), None),
        P(None, ("seq", "trk"), None),
        P(None, ("seq", "trk"), None),
        P(None, ("seq", "trk")),
        P(None, ("seq", "trk")),
        P(None, ("seq", "trk")),
        P(None, ("seq", "trk")),
        P(None, ("seq", "trk")),
        P(None, ("seq", "trk")),
        P(("seq", "trk"), None),
        P(("seq", "trk"), None),
        P(("seq", "trk"), None),
        P(("seq", "trk"), None),
        P(("seq", "trk"), None),
        P(("seq", "trk"), None),
    )
    out_specs = (
        P(("seq", "trk"), None),
        P(("seq", "trk"), None),
        P(("seq", "trk"), None),
        P(("seq", "trk")),
        P(("seq", "trk")),
        P(("seq", "trk")),
        P(None, ("seq", "trk"), None),
        P(None, ("seq", "trk"), None),
        P(None, ("seq", "trk"), None),
        P(None, ("seq", "trk")),
        P(None, ("seq", "trk")),
        P(None, ("seq", "trk")),
        P(None, ("seq", "trk")),
        P(None, ("seq", "trk")),
        P(None, ("seq", "trk")),
        P(("seq", "trk"), None),
        P(("seq", "trk"), None),
        P(("seq", "trk"), None),
        P(("seq", "trk"), None),
        P(("seq", "trk"), None),
        P(("seq", "trk"), None),
        P(),
    )
    return jax.shard_map(body, mesh=mesh, in_specs=in_specs, out_specs=out_specs, check_vma=False)
```
